512 devices in a mesh: tensor: 8 (over z), expert: 64 (over y, x, core).
Axes of the slice: x: 4, y: 8, z: 8, core: 2. Of those that a mesh axis runs over, the one named last changes fastest.
Arguments:
- tokens: bfloat16 [6144, 2560], P(('expert', 'tensor')), may hold values from -6 to 6
- out_grad: bfloat16 [6144, 2560], P(('expert', 'tensor')), may hold values from -6 to 6
- expert_ids: int32 [6144, 6], P(('expert', 'tensor')), may hold values from 0 to 127, as said below
- gate_values: bfloat16 [6144, 6], P(('expert', 'tensor')), may hold values from 0.049804688 to 0.3984375
- gate_weight: bfloat16 [128, 768, 2560], P('expert', 'tensor'), may hold values from -0.125 to 0.125
- up_weight: bfloat16 [128, 768, 2560], P('expert', 'tensor'), may hold values from -0.0625 to 0.0625
- down_weight: bfloat16 [128, 768, 2560], P('expert', 'tensor'), may hold values from -0.109375 to 0.109375
Outputs:
- input_grad: bfloat16 [6144, 2560], P(('expert', 'tensor'))
The draws below stay inside these ranges and needn't reach their ends.
Inputs may be any that keep to these rules, and one draw needn't show every extreme that they name: `expert_ids`: rows form aligned groups of 96 (the tokens of one index of the expert axis). Each row names 6 different experts on five devices of the expert axis, two of them on one device. Within a group, at most 10 rows name experts of one device, and some devices are named by exactly 10 rows.
All inputs are finite; a program needn't handle non-finite values.
Results may differ from the reference program's by a relative error of at most 0.017.
Values may be sent and summed in bfloat16 or wider, within the bound.
No kernel may reach another device: no remote copies, remote signals or barrier semaphores. Data moves between devices by JAX's collectives and lax.ppermute only.
A program may use at most 128 MiB of HBM per device.

```python
import jax
import jax.numpy as jnp
from jax import lax

D = 2560
HID = 768
EXP_DEV = 2
TOPK = 6
EXPERTS = 128
GROUP = 96
TOKENS = 6144
HID_DEV = 96
USED = 48
CAP = 10
N_TENSOR = 8


def draw_expert_ids(key, part):
    key = jax.random.fold_in(key, 11)
    dest_count = EXPERTS // EXP_DEV
    group_count = TOKENS // GROUP

    def one_group(group_key):
        order_key, choice_key, shuffle_key = jax.random.split(group_key, 3)
        dest_order = jax.random.permutation(order_key, dest_count)
        position = (5 * jnp.arange(GROUP)[:, None] + jnp.arange(5)[None, :]) % USED
        chosen = dest_order[position]
        low_choice = jax.random.randint(choice_key, (GROUP, 4), 0, EXP_DEV)
        single = chosen[:, :4] * EXP_DEV + low_choice
        paired = chosen[:, 4:5] * EXP_DEV + jnp.arange(2)[None, :]
        listed = jnp.concatenate([single, paired], axis=1)
        scores = jax.random.randint(shuffle_key, (GROUP, TOPK), 0, 1 << 20) * TOPK + jnp.arange(TOPK)[None, :]
        shuffle = jnp.argsort(scores, axis=1)
        return jnp.take_along_axis(listed, shuffle, axis=1)
    drawn_ids = jax.vmap(one_group)(jax.random.split(key, group_count))
    return drawn_ids.reshape(TOKENS, TOPK).astype(jnp.int32)


def block_levels(rng, extent, pieces, smallest, high):
    level, own = 1.0, jax.random.fold_in(rng, 6)
    for dim, parts in pieces:
        draws = jnp.exp(jax.random.uniform(jax.random.fold_in(own, dim), (parts,), jnp.float32, smallest / len(pieces), high / len(pieces)))
        level = level * jnp.repeat(draws, extent[dim] // parts).reshape([-1 if axis == dim else 1 for axis in range(len(extent))])
    return level


def normal_values(key, dims, deviation, most, cuts=(), kind=jnp.bfloat16):
    level = block_levels(key, dims, cuts, -0.22, 0.18) if cuts else 1.0
    array = jax.random.normal(key, dims, jnp.float32) * deviation * level
    return jnp.minimum(jnp.maximum(array, -most), most).astype(kind)


def setup_inputs(seed: int = 0) -> dict:
    streams_of = jax.random.split(jax.random.key(seed), 8)
    return {
        "tokens": normal_values(streams_of[0], (TOKENS, D), 1.0, 6.0, ((0, 512),)),
        "out_grad": normal_values(streams_of[1], (TOKENS, D), 1.0, 6.0, ((0, 512),)),
        "expert_ids": draw_expert_ids(jax.random.fold_in(streams_of[7], 71), 0),
        "gate_values": jnp.clip(0.049804688 + 0.3486328 * jax.random.uniform(streams_of[3], (TOKENS, TOPK), jnp.float32) ** block_levels(streams_of[3], (TOKENS, TOPK), ((0, 512),), -0.2, 0.2), 0.049804688, 0.3984375).astype(jnp.bfloat16),
        "gate_weight": normal_values(streams_of[4], (EXPERTS, HID, D), D ** -0.5, 0.125, ((0, 64), (1, 8))),
        "up_weight": normal_values(streams_of[5], (EXPERTS, HID, D), (4 * D) ** -0.5, 0.0625, ((0, 64), (1, 8))),
        "down_weight": normal_values(streams_of[6], (EXPERTS, HID, D), (4 * HID) ** -0.5, 0.109375, ((0, 64), (1, 8))),
    }


def reference(tokens, out_grad, expert_ids, gate_values, gate_weight, up_weight, down_weight):
    dest_count = EXPERTS // EXP_DEV
    group_count = TOKENS // GROUP
    grouped = expert_ids.reshape(group_count, GROUP, TOPK)
    dest_ids = grouped // EXP_DEV
    member = jnp.max((dest_ids[:, :, :, None] == jnp.arange(dest_count, dtype=jnp.int32)[None, None, None, :]).astype(jnp.int32), axis=2)
    earlier = jnp.cumsum(member, axis=1) - member
    position = jnp.where(member > 0, earlier, CAP).astype(jnp.int32)
    grid_shape = (group_count, GROUP, dest_count)
    dest_grid = jnp.broadcast_to(jnp.arange(dest_count, dtype=jnp.int32)[None, None, :], grid_shape)
    group_grid = jnp.broadcast_to(jnp.arange(group_count, dtype=jnp.int32)[:, None, None], grid_shape)
    token_grid = jnp.broadcast_to(jnp.arange(TOKENS, dtype=jnp.int32).reshape(group_count, GROUP)[:, :, None], grid_shape)
    table = jnp.full((dest_count, group_count, CAP), TOKENS, jnp.int32)
    table = table.at[dest_grid, group_grid, position].set(token_grid, mode="drop")
    token_rep = jnp.broadcast_to(jnp.arange(TOKENS, dtype=jnp.int32)[:, None], (TOKENS, TOPK))
    weight_table = jnp.zeros((TOKENS + 1, EXPERTS), jnp.float32).at[token_rep, expert_ids].add(gate_values.astype(jnp.float32))
    zero_row = jnp.zeros((1, D), jnp.bfloat16)
    x_padded = jnp.concatenate([tokens, zero_row], axis=0)
    dy_padded = jnp.concatenate([out_grad, zero_row], axis=0)

    def step(total, dest):
        picked = table[dest].reshape(-1)
        row_count = picked.shape[0]
        row_x = x_padded[picked].astype(jnp.float32)
        row_dy = dy_padded[picked].astype(jnp.float32)
        start = (dest * EXP_DEV).astype(jnp.int32)
        w_gate = lax.dynamic_slice_in_dim(gate_weight, start, EXP_DEV, 0).astype(jnp.float32)
        w_up = lax.dynamic_slice_in_dim(up_weight, start, EXP_DEV, 0).astype(jnp.float32)
        w_down = lax.dynamic_slice_in_dim(down_weight, start, EXP_DEV, 0).astype(jnp.float32)
        row_gate = lax.dynamic_slice_in_dim(weight_table[picked], start, EXP_DEV, 1)
        gate_pre = jnp.einsum("rf,ehf->erh", row_x, w_gate)
        up_pre = jnp.einsum("rf,ehf->erh", row_x, w_up)
        back_proj = jnp.einsum("rf,ehf->erh", row_dy, w_down)
        sigmoid_gate = jax.nn.sigmoid(gate_pre)
        scaled = back_proj * jnp.transpose(row_gate)[:, :, None]
        up_grad = lax.optimization_barrier((scaled * gate_pre * sigmoid_gate).astype(jnp.bfloat16)).astype(jnp.float32)
        gate_grad = lax.optimization_barrier((scaled * up_pre * sigmoid_gate * (1.0 + gate_pre * (1.0 - sigmoid_gate))).astype(jnp.bfloat16)).astype(jnp.float32)
        split_gate = gate_grad.reshape(EXP_DEV, row_count, N_TENSOR, HID_DEV)
        split_up = up_grad.reshape(EXP_DEV, row_count, N_TENSOR, HID_DEV)
        part_sum = jnp.einsum("erth,ethf->rtf", split_gate, w_gate.reshape(EXP_DEV, N_TENSOR, HID_DEV, D))
        part_sum = part_sum + jnp.einsum("erth,ethf->rtf", split_up, w_up.reshape(EXP_DEV, N_TENSOR, HID_DEV, D))
        rounded = lax.optimization_barrier(part_sum.astype(jnp.bfloat16)).astype(jnp.float32)
        total = total.at[picked].add(jnp.sum(rounded, axis=1))
        return total, None

    start_total = jnp.zeros((TOKENS + 1, D), jnp.float32)
    total, unused = lax.scan(step, start_total, jnp.arange(dest_count, dtype=jnp.int32))
    return total[:TOKENS].astype(jnp.bfloat16)
```

```python
import jax
import jax.numpy as jnp
from jax import lax
from jax.experimental import pallas as pl
from jax.experimental.pallas import tpu as pltpu
from jax.sharding import PartitionSpec as P

BF = jnp.bfloat16
F32 = jnp.float32
I32 = jnp.int32
D = 2560
OWN = 12
PADDED = 16
NT = 8
NE = 64
NTOK = NT * PADDED
ROWS = NE * 8
HID2 = 192
FA = 1024
FB = (D - FA) // 4
RA = 512
RB = (D - RA) // NT
VMEM = pl.BlockSpec(memory_space=pltpu.VMEM)
LIMIT = 56 * 1024 * 1024


def call(kernel, out_shapes, name, flops=0, moved=0, scratch=()):
    return pl.pallas_call(
        kernel,
        out_shape=out_shapes,
        scratch_shapes=scratch,
        name=name,
        cost_estimate=pl.CostEstimate(flops=flops, bytes_accessed=moved, transcendentals=0),
        compiler_params=pltpu.CompilerParams(vmem_limit_bytes=LIMIT),
    )


def dot(a, b):
    return jnp.dot(a, b, preferred_element_type=F32)


def dot_t(a, b):
    return lax.dot_general(a, b, (((1,), (1,)), ((), ())), preferred_element_type=F32)


def iota(shape, dim):
    return lax.broadcasted_iota(I32, shape, dim)


def start_kernel(x_ref, dy_ref, meta_ref, msg_ref, all_ref):
    msg_ref[...] = jnp.zeros_like(msg_ref)
    all_ref[...] = jnp.zeros_like(all_ref)
    all_ref[0:OWN, 0:D] = x_ref[...]
    all_ref[0:OWN, D : 2 * D] = dy_ref[...]
    for t in range(NT):
        src = x_ref if t < 4 else dy_ref
        low = FA + FB * (t % 4)
        msg_ref[t, 0:OWN, 0:FB] = src[:, low : low + FB]
        msg_ref[t, 0:OWN, FB : FB + 128] = meta_ref[...]


def positions(meta):
    ids = meta.astype(F32).astype(I32)
    lane = iota((NTOK, 128), 1)
    row = iota((NTOK, 128), 0)
    hit = jnp.zeros((NTOK, 128), jnp.bool_)
    for k in range(6):
        hit = hit | ((ids[:, k : k + 1] >> 1) == (lane >> 1))
    member = jnp.where(hit & ((row & 15) < OWN), 1.0, 0.0)
    lower = jnp.where(lane < row, 1.0, 0.0).astype(BF)
    earlier = dot(lower, member.astype(BF))
    return jnp.where(member > 0.5, earlier, -1.0), ids


def one_hots(pos):
    row = iota((ROWS, 128), 0)
    lane = iota((ROWS, 128), 1)
    pick = jnp.where(lane == 2 * (row >> 3), 1.0, 0.0).astype(BF)
    spread = dot_t(pick, pos.astype(BF)).astype(I32)
    sub = row & 7
    main = jnp.where(spread == sub, 1.0, 0.0).astype(BF)
    left = jnp.where(spread == 8 + (sub >> 2), 1.0, 0.0).astype(BF)
    return main, left


def fold(left_rows, tiles, first, sub4):
    out = jnp.zeros((ROWS, 128), F32)
    for k in range(tiles):
        low = 128 * (first + k)
        out = jnp.where(sub4 == k, left_rows[:, low : low + 128], out)
    return out


def pack_b_kernel(msg_ref, out_ref):
    meta = msg_ref[:, FB : FB + 128]
    pos, ids = positions(meta)
    main, left = one_hots(pos)
    values = msg_ref[:, 0:FB]
    out_ref[:, 0:FB] = dot(main, values).astype(BF)
    gates = meta.astype(F32)
    lane = iota((NTOK, 128), 1)
    weight = jnp.zeros((NTOK, 128), F32)
    for k in range(6):
        weight = weight + jnp.where(ids[:, k : k + 1] == lane, gates[:, 6 + k : 7 + k], 0.0)
    weight = weight.astype(BF)
    row16 = iota((16, 128), 0)
    gate_of = jnp.zeros((16, 128), F32)
    for s in range(10):
        col = jnp.sum(jnp.where(pos == float(s), weight.astype(F32), 0.0), axis=0, keepdims=True)
        gate_of = jnp.where(row16 == s, col, gate_of)
    gate_of = jnp.concatenate([gate_of, jnp.zeros((112, 128), F32)], axis=0).astype(BF)
    row = iota((ROWS, 128), 0)
    sub = row & 7
    wide = iota((ROWS, 128), 1)
    pick = jnp.where((wide == 2 * (row >> 3) + (sub >> 2)) & ((sub & 3) == 3), 1.0, 0.0)
    gate_tile = dot_t(pick.astype(BF), gate_of)
    folded = fold(dot(left, values), 3, 0, sub & 3)
    out_ref[:, FB : FB + 128] = jnp.where((sub & 3) == 3, gate_tile, folded).astype(BF)


def pack_a_kernel(msg_ref, x_ref, out_ref):
    pos, _ = positions(msg_ref[:, FB : FB + 128])
    main, left = one_hots(pos)
    sub4 = iota((ROWS, 128), 0) & 3
    for part in range(2):
        values = x_ref[:, part * D : part * D + FA]
        out_ref[:, part * FA : (part + 1) * FA] = dot(main, values).astype(BF)
        spread = dot(left, values)
        for q in range(2):
            low = 2 * FA + (2 * part + q) * 128
            out_ref[:, low : low + 128] = fold(spread, 4, 4 * q, sub4).astype(BF)


def perm(inverse):
    row = iota((ROWS, ROWS), 0)
    col = iota((ROWS, ROWS), 1)
    if inverse:
        row, col = col, row
    return jnp.where(((col & 7) == (row >> 6)) & ((col >> 3) == (row & 63)), 1.0, 0.0).astype(BF)


def compute_kernel(b_ref, a_ref, wg_ref, wu_ref, wd_ref, rs_ref, back_ref, left_ref, z_ref):
    turn = perm(False)
    for q in range(4):
        tile = dot(turn, a_ref[:, 2 * FA + 128 * q : 2 * FA + 128 * (q + 1)]).astype(BF)
        base = (q // 2) * D + (q % 2) * 512
        for s in range(2):
            for k in range(4):
                left_ref[64 * s : 64 * s + 64, base + 128 * k : base + 128 * (k + 1)] = tile[
                    64 * (4 * s + k) : 64 * (4 * s + k + 1)
                ]
    gate_tiles = None
    for t in range(NT):
        tile = dot(turn, b_ref[ROWS * t : ROWS * (t + 1), FB : FB + 128]).astype(BF)
        base = (t // 4) * D + FA + (t % 4) * FB
        if t == 0:
            gate_tiles = (tile[64 * 3 : 64 * 4], tile[64 * 7 : 64 * 8])
        for s in range(2):
            for k in range(3):
                left_ref[64 * s : 64 * s + 64, base + 128 * k : base + 128 * (k + 1)] = tile[
                    64 * (4 * s + k) : 64 * (4 * s + k + 1)
                ]
    wg = wg_ref[...].reshape(HID2, D)
    wu = wu_ref[...].reshape(HID2, D)
    wd = wd_ref[...].reshape(HID2, D)
    row = iota((ROWS, 64), 0)
    spread = jnp.where((row >> 3) == iota((ROWS, 64), 1), 1.0, 0.0).astype(BF)
    wide = iota((ROWS, 128), 1)
    sub = iota((ROWS, 128), 0) & 7
    gate_main = []
    gate_left = []
    for e in range(2):
        both = dot(spread, gate_tiles[e])
        gate_main.append(jnp.sum(jnp.where(wide == sub, both, 0.0), axis=1, keepdims=True))
        own = gate_tiles[e].astype(F32)
        gate_left.append(jnp.concatenate([own[:, 8:9], own[:, 9:10]], axis=0))

    def grads(gate_pre, up_pre, back_proj, gates):
        lane = iota(gate_pre.shape, 1)
        scaled = back_proj * jnp.where(lane < HID2 // 2, gates[0], gates[1])
        sig = 1.0 / (1.0 + jnp.exp(-gate_pre))
        up_grad = (scaled * gate_pre * sig).astype(BF)
        gate_grad = (scaled * up_pre * sig * (1.0 + gate_pre * (1.0 - sig))).astype(BF)
        return gate_grad, up_grad

    gate_pre = dot_t(a_ref[:, 0:FA], wg[:, 0:FA])
    up_pre = dot_t(a_ref[:, 0:FA], wu[:, 0:FA])
    back_proj = dot_t(a_ref[:, FA : 2 * FA], wd[:, 0:FA])
    for t in range(4):
        low = FA + FB * t
        rows = b_ref[ROWS * t : ROWS * (t + 1), 0:FB]
        gate_pre = gate_pre + dot_t(rows, wg[:, low : low + FB])
        up_pre = up_pre + dot_t(rows, wu[:, low : low + FB])
        rows = b_ref[ROWS * (t + 4) : ROWS * (t + 5), 0:FB]
        back_proj = back_proj + dot_t(rows, wd[:, low : low + FB])
    gate_grad, up_grad = grads(gate_pre, up_pre, back_proj, gate_main)
    gate_grad_l, up_grad_l = grads(
        dot_t(left_ref[:, 0:D], wg),
        dot_t(left_ref[:, 0:D], wu),
        dot_t(left_ref[:, D : 2 * D], wd),
        gate_left,
    )
    turn_back = perm(True)
    z_ref[...] = jnp.zeros_like(z_ref)
    for t in range(NT + 1):
        low = 0 if t == NT else RA + RB * t
        width = RA if t == NT else RB
        part = dot(gate_grad, wg[:, low : low + width]) + dot(up_grad, wu[:, low : low + width])
        part_l = dot(gate_grad_l, wg[:, low : low + width]) + dot(up_grad_l, wu[:, low : low + width])
        part_l = part_l.astype(BF)
        for s in range(2):
            for k in range(width // 128):
                z_ref[64 * (4 * s + k) : 64 * (4 * s + k + 1), :] = part_l[
                    64 * s : 64 * s + 64, 128 * k : 128 * (k + 1)
                ]
        folded = dot(turn_back, z_ref[...]).astype(BF)
        if t == NT:
            back_ref[:, 0:RA] = part.astype(BF)
            back_ref[:, RA : RA + 128] = folded
        else:
            rs_ref[t, :, 0:RB] = part.astype(BF)
            rs_ref[t, :, RB : RB + 128] = folded


def combine_kernel(msg_ref, b_ref, a_ref, out_ref):
    pos, _ = positions(msg_ref[:, FB : FB + 128])
    row = iota((128, ROWS), 0)
    col = iota((128, ROWS), 1)
    pick = jnp.where(row == 2 * (col >> 3), 1.0, 0.0).astype(BF)
    spread = dot(pos.astype(BF), pick).astype(I32)
    sub = col & 7
    main = jnp.where(spread == sub, 1.0, 0.0).astype(BF)
    left = spread == 8 + (sub >> 2)
    for k in range(4):
        left_k = jnp.where(left & ((sub & 3) == k), 1.0, 0.0).astype(BF)
        cols = slice(128 * k, 128 * (k + 1))
        total = dot(main, a_ref[:, cols]) + dot(left_k, a_ref[:, RA : RA + 128])
        out_ref[:, cols] = total.astype(BF)
        if k < 2:
            total = dot(main, b_ref[:, cols]) + dot(left_k, b_ref[:, RB : RB + 128])
            out_ref[:, RA + 128 * k : RA + 128 * (k + 1)] = total.astype(BF)


def finish_kernel(in_ref, out_ref):
    total = in_ref[0, :, 0:RA].astype(F32)
    for t in range(1, NT):
        total = total + in_ref[t, :, 0:RA].astype(F32)
    out_ref[:, 0:RA] = total.astype(BF)[0:OWN]
    for t in range(NT):
        low = RA + RB * t
        out_ref[:, low : low + RB] = in_ref[t, 0:OWN, RA : RA + RB]


def per_device(tokens, out_grad, expert_ids, gate_values, gate_weight, up_weight, down_weight):
    meta = jnp.concatenate([expert_ids.astype(BF), gate_values], axis=1)
    meta = jnp.pad(meta, ((0, 0), (0, 128 - meta.shape[1])))
    msg, both = call(
        start_kernel,
        (
            jax.ShapeDtypeStruct((NT, PADDED, FB + 128), BF),
            jax.ShapeDtypeStruct((PADDED, 2 * D), BF),
        ),
        "start",
    )(tokens, out_grad, meta)
    both_all = lax.all_gather(both, "tensor", axis=0, tiled=True)
    msg = lax.all_to_all(msg, "tensor", 0, 0, tiled=True).reshape(NTOK, FB + 128)
    send_b = call(
        pack_b_kernel, jax.ShapeDtypeStruct((ROWS, FB + 128), BF), "pack_b", flops=2 * ROWS * 128 * 1024
    )(msg)
    recv_b = lax.all_to_all(send_b.reshape(NE, 8, FB + 128), "expert", 0, 0, tiled=True)
    all_b = lax.all_gather(recv_b.reshape(ROWS, FB + 128), "tensor", axis=0, tiled=True)
    send_a = call(
        pack_a_kernel,
        jax.ShapeDtypeStruct((ROWS, 2 * FA + 512), BF),
        "pack_a",
        flops=2 * ROWS * 128 * 4096,
    )(msg, both_all)
    recv_a = lax.all_to_all(send_a.reshape(NE, 8, 2 * FA + 512), "expert", 0, 0, tiled=True)
    to_sum, to_send = call(
        compute_kernel,
        (
            jax.ShapeDtypeStruct((NT, ROWS, RB + 128), BF),
            jax.ShapeDtypeStruct((ROWS, RA + 128), BF),
        ),
        "experts",
        flops=10 * 640 * D * HID2,
        moved=16_000_000,
        scratch=[pltpu.VMEM((128, 2 * D), BF), pltpu.VMEM((ROWS, 128), BF)],
    )(all_b, recv_a.reshape(ROWS, 2 * FA + 512), gate_weight, up_weight, down_weight)
    summed = lax.psum_scatter(to_sum, "tensor", scatter_dimension=0, tiled=False)
    back_a = lax.all_to_all(to_send.reshape(NE, 8, RA + 128), "expert", 0, 0, tiled=True)
    back_b = lax.all_to_all(summed.reshape(NE, 8, RB + 128), "expert", 0, 0, tiled=True)
    last = call(
        combine_kernel,
        jax.ShapeDtypeStruct((NTOK, RA + RB), BF),
        "combine",
        flops=2 * ROWS * 128 * 1536,
    )(msg, back_b.reshape(ROWS, RB + 128), back_a.reshape(ROWS, RA + 128))
    last = lax.all_to_all(last.reshape(NT, PADDED, RA + RB), "tensor", 0, 0, tiled=True)
    return call(finish_kernel, jax.ShapeDtypeStruct((OWN, D), BF), "finish")(last)


def solution(mesh):
    return jax.shard_map(
        per_device,
        mesh=mesh,
        in_specs=(
            P(("expert", "tensor"), None),
            P(("expert", "tensor"), None),
            P(("expert", "tensor"), None),
            P(("expert", "tensor"), None),
            P("expert", "tensor", None),
            P("expert", "tensor", None),
            P("expert", "tensor", None),
        ),
        out_specs=P(("expert", "tensor"), None),
        check_vma=False,
    )
```

```python
import jax
import jax.numpy as jnp
from jax import lax
from jax.experimental import pallas as pl
from jax.experimental.pallas import tpu as pltpu
from jax.sharding import PartitionSpec as P

BF = jnp.bfloat16
F32 = jnp.float32
I32 = jnp.int32
D = 2560
OWN = 12
PADDED = 16
NT = 8
NE = 64
NTOK = NT * PADDED
ROWS = NE * 8
HID2 = 192
FA = 512
FB = (D - FA) // 4
LA = 1536
LB = (D - LA) // 4
META = 128
SENT_A = 2 * FA + 2 * 2 * LA // 8
SENT_B = FB + 128
GATHERED = ROWS + NE
RA = 1024
RB = 256
SMALL = 24 * 1024 * 1024
LARGE = 60 * 1024 * 1024


def call(kernel, out_shapes, name, flops=0, moved=0, scratch=(), limit=SMALL):
    return pl.pallas_call(
        kernel,
        out_shape=out_shapes,
        scratch_shapes=scratch,
        name=name,
        cost_estimate=pl.CostEstimate(flops=flops, bytes_accessed=moved, transcendentals=0),
        compiler_params=pltpu.CompilerParams(vmem_limit_bytes=limit),
    )


def dot(a, b):
    return jnp.dot(a, b, preferred_element_type=F32)


def dot_t(a, b):
    return lax.dot_general(a, b, (((1,), (1,)), ((), ())), preferred_element_type=F32)


def iota(shape, dim):
    return lax.broadcasted_iota(I32, shape, dim)


def mask(cond):
    return jnp.where(cond, 1.0, 0.0).astype(BF)


def start_kernel(x_ref, dy_ref, ids_ref, gates_ref, msg_ref, all_ref):
    msg_ref[...] = jnp.zeros_like(msg_ref)
    all_ref[...] = jnp.zeros_like(all_ref)
    all_ref[0:OWN, 0:D] = x_ref[...]
    all_ref[0:OWN, D : 2 * D] = dy_ref[...]
    row = iota((6, META), 0)
    lane = iota((6, META), 1)
    place = [jnp.where(lane == row + 6 * i, 1.0, 0.0).astype(BF) for i in range(2)]
    cols = (((0,), (0,)), ((), ()))
    meta = lax.dot_general(
        ids_ref[...].astype(F32).astype(BF), place[0], cols, preferred_element_type=F32
    ) + lax.dot_general(gates_ref[...], place[1], cols, preferred_element_type=F32)
    meta = meta.astype(BF)
    for t in range(NT):
        src = x_ref if t < 4 else dy_ref
        low = FA + FB * (t % 4)
        msg_ref[t, 0:OWN, 0:FB] = src[:, low : low + FB]
        low = LA + LB * (t % 4)
        msg_ref[t, 0:OWN, FB : FB + LB] = src[:, low : low + LB]
        msg_ref[t, 0:OWN, FB + LB : FB + LB + META] = meta


def positions(meta):
    ids = meta.astype(F32).astype(I32)
    lane = iota((NTOK, 128), 1)
    row = iota((NTOK, 128), 0)
    hit = jnp.zeros((NTOK, 128), jnp.bool_)
    for k in range(6):
        hit = hit | ((ids[:, k : k + 1] >> 1) == (lane >> 1))
    member = jnp.where(hit & ((row & 15) < OWN), 1.0, 0.0)
    lower = jnp.where(lane < row, 1.0, 0.0).astype(BF)
    earlier = dot(lower, member.astype(BF))
    return jnp.where(member > 0.5, earlier, -1.0), ids


def one_hots(pos):
    row = iota((ROWS, 128), 0)
    lane = iota((ROWS, 128), 1)
    pick = jnp.where(lane == 2 * (row >> 3), 1.0, 0.0).astype(BF)
    spread = dot_t(pick, pos.astype(BF)).astype(I32)
    sub = row & 7
    main = jnp.where(spread == sub, 1.0, 0.0).astype(BF)
    left = jnp.where(spread == 8 + (sub >> 2), 1.0, 0.0).astype(BF)
    return main, left


def pack_b_kernel(msg_ref, out_ref):
    meta = msg_ref[:, FB + LB : FB + LB + META]
    pos, ids = positions(meta)
    main, left = one_hots(pos)
    out_ref[:, 0:FB] = dot(main, msg_ref[:, 0:FB]).astype(BF)
    row = iota((ROWS, 128), 0)
    sub = row & 7
    pick = mask(iota((ROWS, 128), 1) == 2 * (row >> 3))
    spread = dot_t(pick, pos.astype(BF)).astype(I32)
    tiles = dot(mask(spread == 8 + (sub >> 1)), msg_ref[:, FB : FB + LB])
    tile = jnp.where((sub & 1) == 0, tiles[:, 0:128], tiles[:, 128:256])
    gates = meta.astype(F32)
    lane = iota((NTOK, 128), 1)
    weight = jnp.zeros((NTOK, 128), F32)
    for k in range(6):
        weight = weight + jnp.where(ids[:, k : k + 1] == lane, gates[:, 6 + k : 7 + k], 0.0)
    row16 = iota((16, 128), 0)
    gate_of = jnp.zeros((16, 128), F32)
    for s in range(10):
        col = jnp.sum(jnp.where(pos == float(s), weight, 0.0), axis=0, keepdims=True)
        gate_of = jnp.where(row16 == s, col, gate_of)
    gate_of = jnp.concatenate([gate_of, jnp.zeros((112, 128), F32)], axis=0).astype(BF)
    pick = mask((iota((ROWS, 128), 1) == 2 * (row >> 3) + (sub & 1)) & ((sub >> 1) == 2))
    out_ref[:, FB : FB + 128] = jnp.where(sub < 4, tile, dot_t(pick, gate_of)).astype(BF)


def unpack_b_kernel(in_ref, out_ref, gate_ref):
    out_ref[0:ROWS, :] = in_ref[:, 0:FB]
    row = iota((ROWS, ROWS), 0)
    col = iota((ROWS, ROWS), 1)
    turn = mask(((col & 7) == (row >> 6)) & ((col >> 3) == (row & 63)))
    turned = dot(turn, in_ref[:, FB : FB + 128])
    for r in range(4):
        out_ref[ROWS : ROWS + 64, 128 * r : 128 * (r + 1)] = turned[64 * r : 64 * (r + 1)].astype(BF)
    spread = mask((iota((ROWS, 64), 0) >> 3) == iota((ROWS, 64), 1))
    wide = iota((ROWS, 128), 1)
    sub = iota((ROWS, 128), 0) & 7
    main = jnp.zeros((ROWS, 128), F32)
    rest = jnp.zeros((128, 128), F32)
    lane = iota((128, 128), 1)
    for e in range(2):
        own = turned[64 * (4 + e) : 64 * (5 + e)]
        both = jnp.where(wide == sub, dot(spread, own.astype(BF)), 0.0)
        main = jnp.where(wide == e, jnp.sum(both, axis=1, keepdims=True), main)
        column = jnp.concatenate([own[:, 8:9], own[:, 9:10]], axis=0)
        rest = jnp.where(lane == e, column, rest)
    gate_ref[0:ROWS, :] = main
    gate_ref[ROWS : ROWS + 128, :] = rest


def pack_a_kernel(msg_ref, x_ref, out_ref):
    pos, _ = positions(msg_ref[:, FB + LB : FB + LB + META])
    main, left = one_hots(pos)
    sub4 = iota((ROWS, 128), 0) & 3
    for part in range(2):
        out_ref[:, part * FA : (part + 1) * FA] = dot(main, x_ref[:, part * D : part * D + FA]).astype(BF)
        for q in range(LA // 512):
            low = part * D + 512 * q
            spread = dot(left, x_ref[:, low : low + 512])
            out = spread[:, 0:128]
            for k in range(1, 4):
                out = jnp.where(sub4 == k, spread[:, 128 * k : 128 * (k + 1)], out)
            low = 2 * FA + 128 * (part * (LA // 512) + q)
            out_ref[:, low : low + 128] = out.astype(BF)


def gathered_kernel(b_ref, wg_ref, wu_ref, wd_ref, gate_ref, up_ref, down_ref, x_ref, y_ref):
    wg = wg_ref[...].reshape(HID2, D)
    wu = wu_ref[...].reshape(HID2, D)
    wd = wd_ref[...].reshape(HID2, D)
    gate_pre = up_pre = back_proj = 0.0
    for t in range(4):
        cols = slice(FA + FB * t, FA + FB * (t + 1))
        x0, y0 = GATHERED * t, GATHERED * (t + 4)
        rows = b_ref[x0 : x0 + ROWS, :]
        gate_pre = gate_pre + dot_t(rows, wg[:, cols])
        up_pre = up_pre + dot_t(rows, wu[:, cols])
        back_proj = back_proj + dot_t(b_ref[y0 : y0 + ROWS, :], wd[:, cols])
        for s in range(2):
            x_ref[64 * s : 64 * s + 64, LB * t : LB * (t + 1)] = b_ref[
                x0 + ROWS : x0 + GATHERED, LB * s : LB * (s + 1)
            ]
            y_ref[64 * s : 64 * s + 64, LB * t : LB * (t + 1)] = b_ref[
                y0 + ROWS : y0 + GATHERED, LB * s : LB * (s + 1)
            ]
    gate_ref[0:ROWS, :] = gate_pre
    up_ref[0:ROWS, :] = up_pre
    down_ref[0:ROWS, :] = back_proj
    gate_ref[ROWS : ROWS + 128, :] = dot_t(x_ref[...], wg[:, LA:D])
    up_ref[ROWS : ROWS + 128, :] = dot_t(x_ref[...], wu[:, LA:D])
    down_ref[ROWS : ROWS + 128, :] = dot_t(y_ref[...], wd[:, LA:D])


def perm(inverse):
    row = iota((ROWS, ROWS), 0)
    col = iota((ROWS, ROWS), 1)
    if inverse:
        row, col = col, row
    return jnp.where(((col & 7) == (row >> 6)) & ((col >> 3) == (row & 63)), 1.0, 0.0).astype(BF)


def grads(gate_pre, up_pre, back_proj, gates):
    lane = iota(gate_pre.shape, 1)
    scaled = back_proj * jnp.where(lane < HID2 // 2, gates[0], gates[1])
    sig = 1.0 / (1.0 + jnp.exp(-gate_pre))
    up_grad = (scaled * gate_pre * sig).astype(BF)
    gate_grad = (scaled * up_pre * sig * (1.0 + gate_pre * (1.0 - sig))).astype(BF)
    return gate_grad, up_grad


def sum_kernel(
    a_ref,
    gates_ref,
    gate_ref,
    up_ref,
    down_ref,
    wg_ref,
    wu_ref,
    wd_ref,
    rs_ref,
    main_ref,
    rest_ref,
    left_ref,
):
    wg = wg_ref[...].reshape(HID2, D)
    wu = wu_ref[...].reshape(HID2, D)
    wd = wd_ref[...].reshape(HID2, D)
    turned = dot(perm(False), a_ref[:, 2 * FA : SENT_A]).astype(BF)
    for q in range(2 * LA // 512):
        for s in range(2):
            for k in range(4):
                left_ref[64 * s : 64 * s + 64, 512 * q + 128 * k : 512 * q + 128 * (k + 1)] = turned[
                    64 * (4 * s + k) : 64 * (4 * s + k + 1), 128 * q : 128 * (q + 1)
                ]
    own = slice(0, ROWS)
    gate_grad, up_grad = grads(
        gate_ref[own, :] + dot_t(a_ref[:, 0:FA], wg[:, 0:FA]),
        up_ref[own, :] + dot_t(a_ref[:, 0:FA], wu[:, 0:FA]),
        down_ref[own, :] + dot_t(a_ref[:, FA : 2 * FA], wd[:, 0:FA]),
        (gates_ref[own, 0:1], gates_ref[own, 1:2]),
    )
    own = slice(ROWS, ROWS + 128)
    gate_left, up_left = grads(
        gate_ref[own, :] + dot_t(left_ref[:, 0:LA], wg[:, 0:LA]),
        up_ref[own, :] + dot_t(left_ref[:, 0:LA], wu[:, 0:LA]),
        down_ref[own, :] + dot_t(left_ref[:, LA : 2 * LA], wd[:, 0:LA]),
        (gates_ref[own, 0:1], gates_ref[own, 1:2]),
    )
    main_ref[0], main_ref[1] = gate_grad, up_grad
    rest_ref[0], rest_ref[1] = gate_left, up_left

    def part(low, width):
        cols = slice(low, low + width)
        return (
            dot(gate_grad, wg[:, cols]) + dot(up_grad, wu[:, cols]),
            dot(gate_left, wg[:, cols]) + dot(up_left, wu[:, cols]),
        )

    row = iota((ROWS, 768), 0)
    col = iota((ROWS, 768), 1)
    sub = row & 7
    first = (col < 512) & ((col >> 3) == (row >> 3)) & (((col & 7) >> 1) == sub)
    rest = (col >= 512) & ((col & 63) == (row >> 3))
    slot = (col >> 6) & 3
    rest = rest & (((slot < 2) & (sub == 4 + slot)) | ((slot >= 2) & (sub == 6)))
    place = jnp.where(first | rest, 1.0, 0.0).astype(BF)

    def halves(tile, odd_rows, odd_slice):
        low_half = iota(tile.shape, 1) < 64
        moved = pltpu.roll(tile, 64, 1)
        both = jnp.where(low_half, moved, tile) if odd_slice else jnp.where(low_half, tile, moved)
        return jnp.where(low_half == odd_rows, 0.0, both).astype(BF)

    odd_main = (iota((ROWS, 128), 0) & 1) == 1
    odd_left = iota((128, 128), 0) >= 64
    for c in range(2):
        half_main, half_left = part(2048 + 256 * c, 256)
        for pair in range(2):
            t0 = 4 * c + 2 * pair
            full_main, full_left = part(RA + 128 * t0, 256)
            tile_main = half_main[:, 128 * pair : 128 * (pair + 1)]
            tile_left = half_left[:, 128 * pair : 128 * (pair + 1)]
            for i in range(2):
                stack = jnp.concatenate(
                    [
                        halves(tile_main, odd_main, i == 1),
                        full_left[:, 128 * i : 128 * (i + 1)].astype(BF),
                        halves(tile_left, odd_left, i == 1),
                    ],
                    axis=0,
                )
                rs_ref[t0 + i, :, 0:128] = full_main[:, 128 * i : 128 * (i + 1)].astype(BF)
                rs_ref[t0 + i, :, 128:256] = dot(place, stack).astype(BF)


def direct_kernel(main_ref, rest_ref, wg_ref, wu_ref, out_ref, z_ref):
    wg = wg_ref[...].reshape(HID2, D)
    wu = wu_ref[...].reshape(HID2, D)
    out_ref[:, 0:RA] = (dot(main_ref[0], wg[:, 0:RA]) + dot(main_ref[1], wu[:, 0:RA])).astype(BF)
    part = (dot(rest_ref[0], wg[:, 0:RA]) + dot(rest_ref[1], wu[:, 0:RA])).astype(BF)
    for q in range(RA // 512):
        for s in range(2):
            for k in range(4):
                low = 512 * q + 128 * k
                z_ref[64 * (4 * s + k) : 64 * (4 * s + k + 1), 128 * q : 128 * (q + 1)] = part[
                    64 * s : 64 * s + 64, low : low + 128
                ]
    out_ref[:, RA : RA + RA // 4] = dot(perm(True), z_ref[...]).astype(BF)


def spread_positions(msg_ref):
    pos, _ = positions(msg_ref[:, FB + LB : FB + LB + META])
    row = iota((128, ROWS), 0)
    col = iota((128, ROWS), 1)
    pick = jnp.where(row == 2 * (col >> 3), 1.0, 0.0).astype(BF)
    return dot(pos.astype(BF), pick).astype(I32), col & 7


def combine_a_kernel(msg_ref, a_ref, out_ref):
    spread, sub = spread_positions(msg_ref)
    main = mask(spread == sub)
    total = dot(main, a_ref[:, 0:RA])
    for k in range(4):
        left = mask((spread == 8 + (sub >> 2)) & ((sub & 3) == k))
        rest = dot(left, a_ref[:, RA : RA + RA // 4])
        for q in range(RA // 512):
            low = 512 * q + 128 * k
            out_ref[:, low : low + 128] = (
                total[:, low : low + 128] + rest[:, 128 * q : 128 * (q + 1)]
            ).astype(BF)


def combine_b_kernel(msg_ref, b_ref, a_ref, out_ref):
    spread, sub = spread_positions(msg_ref)
    out_ref[:, 0:RA] = a_ref[...]
    main = mask(spread == sub)
    tile = b_ref[:, 128:256]
    rest = mask(((sub == 4) & (spread == 8)) | ((sub == 5) & (spread == 9)))
    out_ref[:, RA : RA + 128] = (dot(main, b_ref[:, 0:128]) + dot(rest, tile)).astype(BF)
    low = dot(mask(((sub < 4) & (spread == 2 * sub)) | ((sub == 6) & (spread == 8))), tile)
    high = dot(mask(((sub < 4) & (spread == 2 * sub + 1)) | ((sub == 6) & (spread == 9))), tile)
    both = jnp.where(iota((NTOK, 128), 1) < 64, low, high)
    out_ref[:, RA + 128 : RA + 256] = (both + pltpu.roll(both, 64, 1)).astype(BF)


def finish_kernel(in_ref, out_ref):
    total = in_ref[0, :, 0:RA].astype(F32)
    for t in range(1, NT):
        total = total + in_ref[t, :, 0:RA].astype(F32)
    out_ref[:, 0:RA] = total.astype(BF)[0:OWN]
    for t in range(NT):
        low = RA + 128 * t
        out_ref[:, low : low + 128] = in_ref[t, 0:OWN, RA : RA + 128]
    low_half = iota((PADDED, 128), 1) < 64
    for t in range(0, NT, 2):
        low = 2048 + 64 * t
        tile = jnp.where(
            low_half,
            in_ref[t, :, RA + 128 : RA + 256].astype(F32),
            in_ref[t + 1, :, RA + 128 : RA + 256].astype(F32),
        )
        out_ref[:, low : low + 128] = tile.astype(BF)[0:OWN]


def shape(*dims, dtype=BF):
    return jax.ShapeDtypeStruct(dims, dtype)


def per_device(tokens, out_grad, expert_ids, gate_values, gate_weight, up_weight, down_weight):
    weights = (gate_weight, up_weight, down_weight)
    lanes = FB + LB + META
    msg, both = call(start_kernel, (shape(NT, PADDED, lanes), shape(PADDED, 2 * D)), "start", limit=LARGE)(
        tokens, out_grad, expert_ids.T, gate_values.T
    )
    both_all = lax.all_gather(both, "tensor", axis=0, tiled=True)
    msg = lax.all_to_all(msg, "tensor", 0, 0, tiled=True).reshape(NTOK, lanes)
    send_b = call(pack_b_kernel, shape(ROWS, SENT_B), "pack_b", flops=2 * ROWS * 128 * 1280)(msg)
    recv_b = lax.all_to_all(send_b.reshape(NE, 8, SENT_B), "expert", 0, 0, tiled=True)
    own_b, gates = call(
        unpack_b_kernel,
        (shape(GATHERED, FB), shape(ROWS + 128, 128, dtype=F32)),
        "unpack_b",
        flops=2 * ROWS * ROWS * 128,
    )(recv_b.reshape(ROWS, SENT_B))
    all_b = lax.all_gather(own_b, "tensor", axis=0, tiled=True)
    send_a = call(pack_a_kernel, shape(ROWS, SENT_A), "pack_a", flops=2 * ROWS * 128 * 4096)(msg, both_all)
    recv_a = lax.all_to_all(send_a.reshape(NE, 8, SENT_A), "expert", 0, 0, tiled=True)
    pre = call(
        gathered_kernel,
        (shape(ROWS + 128, HID2, dtype=F32),) * 3,
        "gathered",
        flops=6 * ROWS * 2048 * HID2,
        moved=8_000_000,
        scratch=[pltpu.VMEM((128, D - LA), BF), pltpu.VMEM((128, D - LA), BF)],
        limit=LARGE,
    )(all_b, *weights)
    to_sum, main, rest = call(
        sum_kernel,
        (shape(NT, ROWS, RB), shape(2, ROWS, HID2), shape(2, 128, HID2)),
        "sum",
        flops=6 * 640 * D * HID2,
        moved=10_000_000,
        scratch=[pltpu.VMEM((128, 2 * LA), BF)],
        limit=LARGE,
    )(recv_a.reshape(ROWS, SENT_A), gates, *pre, *weights)
    summed = lax.psum_scatter(to_sum, "tensor", scatter_dimension=0, tiled=False)
    to_send = call(
        direct_kernel,
        shape(ROWS, RA + RA // 4),
        "direct",
        flops=4 * 640 * RA * HID2,
        moved=4_000_000,
        scratch=[pltpu.VMEM((ROWS, RA // 4), BF)],
        limit=LARGE,
    )(main, rest, gate_weight, up_weight)
    back_a = lax.all_to_all(to_send.reshape(NE, 8, RA + RA // 4), "expert", 0, 0, tiled=True)
    back_b = lax.all_to_all(summed.reshape(NE, 8, RB), "expert", 0, 0, tiled=True)
    part_a = call(combine_a_kernel, shape(NTOK, RA), "combine_a", flops=2 * ROWS * 128 * 2048)(
        msg, back_a.reshape(ROWS, RA + RA // 4)
    )
    last = call(combine_b_kernel, shape(NTOK, RA + RB), "combine_b", flops=2 * ROWS * 128 * 512)(
        msg, back_b.reshape(ROWS, RB), part_a
    )
    last = lax.all_to_all(last.reshape(NT, PADDED, RA + RB), "tensor", 0, 0, tiled=True)
    return call(finish_kernel, shape(OWN, D), "finish")(last)


def solution(mesh):
    return jax.shard_map(
        per_device,
        mesh=mesh,
        in_specs=(
            P(("expert", "tensor"), None),
            P(("expert", "tensor"), None),
            P(("expert", "tensor"), None),
            P(("expert", "tensor"), None),
            P("expert", "tensor", None),
            P("expert", "tensor", None),
            P("expert", "tensor", None),
        ),
        out_specs=P(("expert", "tensor"), None),
        check_vma=False,
    )
```

```python
import jax
import jax.numpy as jnp
from jax import lax
from jax.experimental import pallas as pl
from jax.experimental.pallas import tpu as pltpu
from jax.sharding import PartitionSpec as P

BF = jnp.bfloat16
F32 = jnp.float32
I32 = jnp.int32
D = 2560
OWN = 12
PADDED = 16
NT = 8
NE = 64
NTOK = NT * PADDED
ROWS = NE * 8
HID2 = 192
FA = 512
FB = (D - FA) // 4
LA = 1536
LB = (D - LA) // 4
META = 128
SENT_A = 2 * FA + 2 * 2 * LA // 8
SENT_B = FB + 128
GATHERED = ROWS + NE
RA = 1024
RB = 256
SMALL = 24 * 1024 * 1024
LARGE = 60 * 1024 * 1024


HBM = pl.BlockSpec(memory_space=pltpu.HBM)
VMEM = pl.BlockSpec(memory_space=pltpu.VMEM)


def call(kernel, out_shapes, name, flops=0, moved=0, scratch=(), limit=SMALL, ins=None, outs=None):
    specs = {}
    if ins is not None:
        specs["in_specs"] = ins
    if outs is not None:
        specs["out_specs"] = outs
    return pl.pallas_call(
        kernel,
        out_shape=out_shapes,
        **specs,
        scratch_shapes=scratch,
        name=name,
        cost_estimate=pl.CostEstimate(flops=flops, bytes_accessed=moved, transcendentals=0),
        compiler_params=pltpu.CompilerParams(vmem_limit_bytes=limit),
    )


def dot(a, b):
    return jnp.dot(a, b, preferred_element_type=F32)


def dot_t(a, b):
    return lax.dot_general(a, b, (((1,), (1,)), ((), ())), preferred_element_type=F32)


def iota(shape, dim):
    return lax.broadcasted_iota(I32, shape, dim)


def mask(cond):
    return jnp.where(cond, 1.0, 0.0).astype(BF)


def start_kernel(x_ref, dy_ref, ids_ref, gates_ref, msg_ref, all_ref):
    msg_ref[...] = jnp.zeros_like(msg_ref)
    all_ref[...] = jnp.zeros_like(all_ref)
    all_ref[0:OWN, 0:D] = x_ref[...]
    all_ref[0:OWN, D : 2 * D] = dy_ref[...]
    row = iota((6, META), 0)
    lane = iota((6, META), 1)
    place = [jnp.where(lane == row + 6 * i, 1.0, 0.0).astype(BF) for i in range(2)]
    cols = (((0,), (0,)), ((), ()))
    meta = lax.dot_general(
        ids_ref[...].astype(F32).astype(BF), place[0], cols, preferred_element_type=F32
    ) + lax.dot_general(gates_ref[...], place[1], cols, preferred_element_type=F32)
    meta = meta.astype(BF)
    for t in range(NT):
        src = x_ref if t < 4 else dy_ref
        low = FA + FB * (t % 4)
        msg_ref[t, 0:OWN, 0:FB] = src[:, low : low + FB]
        low = LA + LB * (t % 4)
        msg_ref[t, 0:OWN, FB : FB + LB] = src[:, low : low + LB]
        msg_ref[t, 0:OWN, FB + LB : FB + LB + META] = meta


def positions(meta):
    ids = meta.astype(F32).astype(I32)
    lane = iota((NTOK, 128), 1)
    row = iota((NTOK, 128), 0)
    hit = jnp.zeros((NTOK, 128), jnp.bool_)
    for k in range(6):
        hit = hit | ((ids[:, k : k + 1] >> 1) == (lane >> 1))
    member = jnp.where(hit & ((row & 15) < OWN), 1.0, 0.0)
    lower = jnp.where(lane < row, 1.0, 0.0).astype(BF)
    earlier = dot(lower, member.astype(BF))
    return jnp.where(member > 0.5, earlier, -1.0), ids


def one_hots(pos):
    row = iota((ROWS, 128), 0)
    lane = iota((ROWS, 128), 1)
    pick = jnp.where(lane == 2 * (row >> 3), 1.0, 0.0).astype(BF)
    spread = dot_t(pick, pos.astype(BF)).astype(I32)
    sub = row & 7
    main = jnp.where(spread == sub, 1.0, 0.0).astype(BF)
    left = jnp.where(spread == 8 + (sub >> 2), 1.0, 0.0).astype(BF)
    return main, left


def pack_b_kernel(msg_ref, out_ref):
    meta = msg_ref[:, FB + LB : FB + LB + META]
    pos, ids = positions(meta)
    main, left = one_hots(pos)
    out_ref[:, 0:FB] = dot(main, msg_ref[:, 0:FB]).astype(BF)
    row = iota((ROWS, 128), 0)
    sub = row & 7
    pick = mask(iota((ROWS, 128), 1) == 2 * (row >> 3))
    spread = dot_t(pick, pos.astype(BF)).astype(I32)
    tiles = dot(mask(spread == 8 + (sub >> 1)), msg_ref[:, FB : FB + LB])
    tile = jnp.where((sub & 1) == 0, tiles[:, 0:128], tiles[:, 128:256])
    gates = meta.astype(F32)
    lane = iota((NTOK, 128), 1)
    weight = jnp.zeros((NTOK, 128), F32)
    for k in range(6):
        weight = weight + jnp.where(ids[:, k : k + 1] == lane, gates[:, 6 + k : 7 + k], 0.0)
    row16 = iota((16, 128), 0)
    gate_of = jnp.zeros((16, 128), F32)
    for s in range(10):
        col = jnp.sum(jnp.where(pos == float(s), weight, 0.0), axis=0, keepdims=True)
        gate_of = jnp.where(row16 == s, col, gate_of)
    gate_of = jnp.concatenate([gate_of, jnp.zeros((112, 128), F32)], axis=0).astype(BF)
    pick = mask((iota((ROWS, 128), 1) == 2 * (row >> 3) + (sub & 1)) & ((sub >> 1) == 2))
    out_ref[:, FB : FB + 128] = jnp.where(sub < 4, tile, dot_t(pick, gate_of)).astype(BF)


def unpack_b_kernel(in_ref, out_ref, gate_out, gate_ref, sem):
    out_ref[0:ROWS, :] = in_ref[:, 0:FB]
    turn = perm(False)
    turned = [dot(turn, in_ref[256 * h : 256 * (h + 1), FB : FB + 128]) for h in range(2)]
    turned = jnp.concatenate([turned[h][32 * r : 32 * (r + 1)] for r in range(6) for h in range(2)], axis=0)
    for r in range(4):
        out_ref[ROWS : ROWS + 64, 128 * r : 128 * (r + 1)] = turned[64 * r : 64 * (r + 1)].astype(BF)
    spread = mask((iota((ROWS, 64), 0) >> 3) == iota((ROWS, 64), 1))
    wide = iota((ROWS, 128), 1)
    sub = iota((ROWS, 128), 0) & 7
    main = jnp.zeros((ROWS, 128), F32)
    rest = jnp.zeros((128, 128), F32)
    lane = iota((128, 128), 1)
    for e in range(2):
        own = turned[64 * (4 + e) : 64 * (5 + e)]
        both = jnp.where(wide == sub, dot(spread, own.astype(BF)), 0.0)
        main = jnp.where(wide == e, jnp.sum(both, axis=1, keepdims=True), main)
        column = jnp.concatenate([own[:, 8:9], own[:, 9:10]], axis=0)
        rest = jnp.where(lane == e, column, rest)
    gate_ref[0:ROWS, :] = main
    gate_ref[ROWS : ROWS + 128, :] = rest
    copy = pltpu.make_async_copy(gate_ref, gate_out, sem)
    copy.start()
    copy.wait()


def pack_a_kernel(msg_ref, x_in, out_ref, x_ref, sem):
    copy = pltpu.make_async_copy(x_in, x_ref, sem)
    copy.start()
    pos, _ = positions(msg_ref[:, FB + LB : FB + LB + META])
    main, left = one_hots(pos)
    sub4 = iota((ROWS, 128), 0) & 3
    copy.wait()
    for part in range(2):
        out_ref[:, part * FA : (part + 1) * FA] = dot(main, x_ref[:, part * D : part * D + FA]).astype(BF)
        for q in range(LA // 512):
            low = part * D + 512 * q
            spread = dot(left, x_ref[:, low : low + 512])
            out = spread[:, 0:128]
            for k in range(1, 4):
                out = jnp.where(sub4 == k, spread[:, 128 * k : 128 * (k + 1)], out)
            low = 2 * FA + 128 * (part * (LA // 512) + q)
            out_ref[:, low : low + 128] = out.astype(BF)


def perm(inverse):
    row = iota((256, 256), 0)
    col = iota((256, 256), 1)
    if inverse:
        row, col = col, row
    return mask(((col & 7) == (row >> 5)) & ((col >> 3) == (row & 31)))


def grads(gate_pre, up_pre, back_proj, gates):
    lane = iota(gate_pre.shape, 1)
    scaled = back_proj * jnp.where(lane < HID2 // 2, gates[0], gates[1])
    sig = 1.0 / (1.0 + jnp.exp(-gate_pre))
    up_grad = (scaled * gate_pre * sig).astype(BF)
    gate_grad = (scaled * up_pre * sig * (1.0 + gate_pre * (1.0 - sig))).astype(BF)
    return gate_grad, up_grad


def experts_kernel(
    a_in,
    b_in,
    gates_in,
    wg_in,
    wu_in,
    wd_in,
    rs_out,
    send_ref,
    a_ref,
    b_ref,
    gates_ref,
    wg_ref,
    wu_ref,
    wd_ref,
    left_ref,
    z_ref,
    rs_ref,
    sems,
    out_sems,
):
    pairs = [(wg_in, wg_ref), (wu_in, wu_ref), (wd_in, wd_ref), (a_in, a_ref), (gates_in, gates_ref)]
    for t in (0, 4, 1, 5, 2, 6, 3, 7):
        rows = pl.ds(GATHERED * t, GATHERED)
        pairs.append((b_in.at[rows], b_ref.at[rows]))
    copies = [pltpu.make_async_copy(src, dst, sems.at[i]) for i, (src, dst) in enumerate(pairs)]
    for copy in copies:
        copy.start()
    turn = perm(False)
    turn_back = perm(True)
    for copy in copies[:4]:
        copy.wait()
    wg = wg_ref[...].reshape(HID2, D)
    wu = wu_ref[...].reshape(HID2, D)
    wd = wd_ref[...].reshape(HID2, D)
    for h in range(2):
        turned = dot(turn, a_ref[256 * h : 256 * (h + 1), 2 * FA : SENT_A]).astype(BF)
        for q in range(2 * LA // 512):
            base = (q // (LA // 512)) * D + 512 * (q % (LA // 512))
            for s in range(2):
                for k in range(4):
                    low = 64 * s + 32 * h
                    left_ref[low : low + 32, base + 128 * k : base + 128 * (k + 1)] = turned[
                        32 * (4 * s + k) : 32 * (4 * s + k + 1), 128 * q : 128 * (q + 1)
                    ]
    gate_pre = dot_t(a_ref[:, 0:FA], wg[:, 0:FA])
    up_pre = dot_t(a_ref[:, 0:FA], wu[:, 0:FA])
    back_proj = dot_t(a_ref[:, FA : 2 * FA], wd[:, 0:FA])
    copies[4].wait()
    for t in range(4):
        copies[5 + 2 * t].wait()
        copies[6 + 2 * t].wait()
        cols = slice(FA + FB * t, FA + FB * (t + 1))
        x0, y0 = GATHERED * t, GATHERED * (t + 4)
        rows = b_ref[x0 : x0 + ROWS, :]
        gate_pre = gate_pre + dot_t(rows, wg[:, cols])
        up_pre = up_pre + dot_t(rows, wu[:, cols])
        back_proj = back_proj + dot_t(b_ref[y0 : y0 + ROWS, :], wd[:, cols])
        for base, start in ((0, x0), (D, y0)):
            low = base + LA + LB * t
            for s in range(2):
                left_ref[64 * s : 64 * s + 64, low : low + LB] = b_ref[
                    start + ROWS : start + GATHERED, LB * s : LB * (s + 1)
                ]
    gate_left, up_left = grads(
        dot_t(left_ref[:, 0:D], wg),
        dot_t(left_ref[:, 0:D], wu),
        dot_t(left_ref[:, D : 2 * D], wd),
        (gates_ref[ROWS : ROWS + 128, 0:1], gates_ref[ROWS : ROWS + 128, 1:2]),
    )
    gate_grad, up_grad = grads(
        gate_pre, up_pre, back_proj, (gates_ref[0:ROWS, 0:1], gates_ref[0:ROWS, 1:2])
    )

    def part(low, width):
        cols = slice(low, low + width)
        return (
            dot(gate_grad, wg[:, cols]) + dot(up_grad, wu[:, cols]),
            dot(gate_left, wg[:, cols]) + dot(up_left, wu[:, cols]),
        )

    row = iota((256, 256), 0)
    col = iota((256, 256), 1)
    place_main = mask(((col >> 3) == (row >> 3)) & (((col & 7) >> 1) == (row & 7)))
    row = iota((ROWS, 256), 0)
    col = iota((ROWS, 256), 1)
    sub = row & 7
    slot = col >> 6
    fits = ((slot < 2) & (sub == 4 + slot)) | ((slot >= 2) & (sub == 6))
    place_left = mask(((col & 63) == (row >> 3)) & fits)

    def halves(tile, odd_rows, odd_slice):
        low_half = iota(tile.shape, 1) < 64
        moved = pltpu.roll(tile, 64, 1)
        both = jnp.where(low_half, moved, tile) if odd_slice else jnp.where(low_half, tile, moved)
        return jnp.where(low_half == odd_rows, 0.0, both).astype(BF)

    odd_main = (iota((ROWS, 128), 0) & 1) == 1
    odd_left = iota((128, 128), 0) >= 64
    outs = []
    for c in range(2):
        half_main, half_left = part(2048 + 256 * c, 256)
        for pair in range(2):
            t0 = 4 * c + 2 * pair
            full_main, full_left = part(RA + 128 * t0, 256)
            tile_main = half_main[:, 128 * pair : 128 * (pair + 1)]
            tile_left = half_left[:, 128 * pair : 128 * (pair + 1)]
            mains = jnp.concatenate([halves(tile_main, odd_main, i == 1) for i in range(2)], axis=1)
            lefts = jnp.concatenate(
                [
                    full_left.astype(BF),
                    jnp.concatenate([halves(tile_left, odd_left, i == 1) for i in range(2)], axis=1),
                ],
                axis=0,
            )
            placed = dot(place_left, lefts)
            for h in range(2):
                rows = slice(256 * h, 256 * (h + 1))
                both = (placed[rows] + dot(place_main, mains[rows])).astype(BF)
                for i in range(2):
                    rs_ref[t0 + i, rows, 128:256] = both[:, 128 * i : 128 * (i + 1)]
            for i in range(2):
                rs_ref[t0 + i, :, 0:128] = full_main[:, 128 * i : 128 * (i + 1)].astype(BF)
                outs.append(pltpu.make_async_copy(rs_ref.at[t0 + i], rs_out.at[t0 + i], out_sems.at[t0 + i]))
                outs[-1].start()
    for q in range(RA // 512):
        sums, rest = part(512 * q, 512)
        send_ref[:, 512 * q : 512 * (q + 1)] = sums.astype(BF)
        rest = rest.astype(BF)
        for h in range(2):
            for s in range(2):
                for k in range(4):
                    low = 32 * (4 * s + k)
                    z_ref[256 * h + low : 256 * h + low + 32, 128 * q : 128 * (q + 1)] = rest[
                        64 * s + 32 * h : 64 * s + 32 * h + 32, 128 * k : 128 * (k + 1)
                    ]
    for h in range(2):
        rows = slice(256 * h, 256 * (h + 1))
        send_ref[rows, RA : RA + RA // 4] = dot(turn_back, z_ref[rows, :]).astype(BF)
    for copy in outs:
        copy.wait()


def spread_positions(msg_ref):
    pos, _ = positions(msg_ref[:, FB + LB : FB + LB + META])
    row = iota((128, ROWS), 0)
    col = iota((128, ROWS), 1)
    pick = jnp.where(row == 2 * (col >> 3), 1.0, 0.0).astype(BF)
    return dot(pos.astype(BF), pick).astype(I32), col & 7


def combine_a_kernel(msg_ref, a_ref, out_ref):
    spread, sub = spread_positions(msg_ref)
    main = mask(spread == sub)
    total = dot(main, a_ref[:, 0:RA])
    for k in range(4):
        left = mask((spread == 8 + (sub >> 2)) & ((sub & 3) == k))
        rest = dot(left, a_ref[:, RA : RA + RA // 4])
        for q in range(RA // 512):
            low = 512 * q + 128 * k
            out_ref[:, low : low + 128] = (
                total[:, low : low + 128] + rest[:, 128 * q : 128 * (q + 1)]
            ).astype(BF)


def combine_b_kernel(msg_ref, b_ref, a_ref, out_ref):
    spread, sub = spread_positions(msg_ref)
    out_ref[:, 0:RA] = a_ref[...]
    main = mask(spread == sub)
    tile = b_ref[:, 128:256]
    rest = mask(((sub == 4) & (spread == 8)) | ((sub == 5) & (spread == 9)))
    out_ref[:, RA : RA + 128] = (dot(main, b_ref[:, 0:128]) + dot(rest, tile)).astype(BF)
    low = dot(mask(((sub < 4) & (spread == 2 * sub)) | ((sub == 6) & (spread == 8))), tile)
    high = dot(mask(((sub < 4) & (spread == 2 * sub + 1)) | ((sub == 6) & (spread == 9))), tile)
    both = jnp.where(iota((NTOK, 128), 1) < 64, low, high)
    out_ref[:, RA + 128 : RA + 256] = (both + pltpu.roll(both, 64, 1)).astype(BF)


def finish_kernel(in_ref, out_ref):
    total = in_ref[0, :, 0:RA].astype(F32)
    for t in range(1, NT):
        total = total + in_ref[t, :, 0:RA].astype(F32)
    out_ref[:, 0:RA] = total.astype(BF)[0:OWN]
    for t in range(NT):
        low = RA + 128 * t
        out_ref[:, low : low + 128] = in_ref[t, 0:OWN, RA : RA + 128]
    low_half = iota((PADDED, 128), 1) < 64
    for t in range(0, NT, 2):
        low = 2048 + 64 * t
        tile = jnp.where(
            low_half,
            in_ref[t, :, RA + 128 : RA + 256].astype(F32),
            in_ref[t + 1, :, RA + 128 : RA + 256].astype(F32),
        )
        out_ref[:, low : low + 128] = tile.astype(BF)[0:OWN]


def shape(*dims, dtype=BF):
    return jax.ShapeDtypeStruct(dims, dtype)


def per_device(tokens, out_grad, expert_ids, gate_values, gate_weight, up_weight, down_weight):
    weights = (gate_weight, up_weight, down_weight)
    lanes = FB + LB + META
    msg, both = call(start_kernel, (shape(NT, PADDED, lanes), shape(PADDED, 2 * D)), "start", limit=LARGE)(
        tokens, out_grad, expert_ids.T, gate_values.T
    )
    both_all = lax.all_gather(both, "tensor", axis=0, tiled=True)
    msg = lax.all_to_all(msg, "tensor", 0, 0, tiled=True).reshape(NTOK, lanes)
    send_b = call(pack_b_kernel, shape(ROWS, SENT_B), "pack_b", flops=2 * ROWS * 128 * 1280)(msg)
    recv_b = lax.all_to_all(send_b.reshape(NE, 8, SENT_B), "expert", 0, 0, tiled=True)
    own_b, gates = call(
        unpack_b_kernel,
        (shape(GATHERED, FB), shape(ROWS + 128, 128, dtype=F32)),
        "unpack_b",
        flops=2 * ROWS * ROWS * 128,
        scratch=[pltpu.VMEM((ROWS + 128, 128), F32), pltpu.SemaphoreType.DMA],
        outs=(VMEM, HBM),
    )(recv_b.reshape(ROWS, SENT_B))
    all_b = lax.all_gather(own_b, "tensor", axis=0, tiled=True)
    send_a = call(
        pack_a_kernel,
        shape(ROWS, SENT_A),
        "pack_a",
        flops=2 * ROWS * 128 * 4096,
        scratch=[pltpu.VMEM((NTOK, 2 * D), BF), pltpu.SemaphoreType.DMA],
        ins=[VMEM, HBM],
    )(msg, both_all)
    recv_a = lax.all_to_all(send_a.reshape(NE, 8, SENT_A), "expert", 0, 0, tiled=True)
    to_sum, to_send = call(
        experts_kernel,
        (shape(NT, ROWS, RB), shape(ROWS, RA + RA // 4)),
        "experts",
        flops=10 * 640 * D * HID2,
        moved=13_000_000,
        scratch=[
            pltpu.VMEM((ROWS, SENT_A), BF),
            pltpu.VMEM((NT * GATHERED, FB), BF),
            pltpu.VMEM((ROWS + 128, 128), F32),
            pltpu.VMEM((2, HID2 // 2, D), BF),
            pltpu.VMEM((2, HID2 // 2, D), BF),
            pltpu.VMEM((2, HID2 // 2, D), BF),
            pltpu.VMEM((128, 2 * D), BF),
            pltpu.VMEM((ROWS, RA // 4), BF),
            pltpu.VMEM((NT, ROWS, RB), BF),
            pltpu.SemaphoreType.DMA((5 + NT,)),
            pltpu.SemaphoreType.DMA((NT,)),
        ],
        limit=LARGE,
        ins=[HBM] * 6,
        outs=(HBM, VMEM),
    )(recv_a.reshape(ROWS, SENT_A), all_b, gates, *weights)
    summed = lax.psum_scatter(to_sum, "tensor", scatter_dimension=0, tiled=False)
    back_a = lax.all_to_all(to_send.reshape(NE, 8, RA + RA // 4), "expert", 0, 0, tiled=True)
    back_b = lax.all_to_all(summed.reshape(NE, 8, RB), "expert", 0, 0, tiled=True)
    part_a = call(combine_a_kernel, shape(NTOK, RA), "combine_a", flops=2 * ROWS * 128 * 2048)(
        msg, back_a.reshape(ROWS, RA + RA // 4)
    )
    last = call(combine_b_kernel, shape(NTOK, RA + RB), "combine_b", flops=2 * ROWS * 128 * 512)(
        msg, back_b.reshape(ROWS, RB), part_a
    )
    last = lax.all_to_all(last.reshape(NT, PADDED, RA + RB), "tensor", 0, 0, tiled=True)
    return call(finish_kernel, shape(OWN, D), "finish")(last)


def solution(mesh):
    return jax.shard_map(
        per_device,
        mesh=mesh,
        in_specs=(
            P(("expert", "tensor"), None),
            P(("expert", "tensor"), None),
            P(("expert", "tensor"), None),
            P(("expert", "tensor"), None),
            P("expert", "tensor", None),
            P("expert", "tensor", None),
            P("expert", "tensor", None),
        ),
        out_specs=P(("expert", "tensor"), None),
        check_vma=False,
    )
```

```python
import jax
import jax.numpy as jnp
from jax import lax
from jax.experimental import pallas as pl
from jax.experimental.pallas import tpu as pltpu
from jax.sharding import PartitionSpec as P

BF = jnp.bfloat16
F32 = jnp.float32
I32 = jnp.int32
D = 2560
OWN = 12
PADDED = 16
NT = 8
NE = 64
NTOK = NT * PADDED
ROWS = NE * 8
HID2 = 192
FA = 512
FB = (D - FA) // 4
LA = 1536
LB = (D - LA) // 4
META = 128
SENT_A = 2 * FA + 2 * 2 * LA // 8
SENT_B = FB + 128
GATHERED = ROWS + NE
RA = 1024
RB = 256
BACK_A = RA + 128
LAST = RA + RB
LAST_PACKED = LAST * 3 // 2
SMALL = 24 * 1024 * 1024
LARGE = 60 * 1024 * 1024


HBM = pl.BlockSpec(memory_space=pltpu.HBM)
VMEM = pl.BlockSpec(memory_space=pltpu.VMEM)


def call(kernel, out_shapes, name, flops=0, moved=0, scratch=(), limit=SMALL, ins=None, outs=None):
    specs = {}
    if ins is not None:
        specs["in_specs"] = ins
    if outs is not None:
        specs["out_specs"] = outs
    return pl.pallas_call(
        kernel,
        out_shape=out_shapes,
        **specs,
        scratch_shapes=scratch,
        name=name,
        cost_estimate=pl.CostEstimate(flops=flops, bytes_accessed=moved, transcendentals=0),
        compiler_params=pltpu.CompilerParams(vmem_limit_bytes=limit),
    )


def dot(a, b):
    return jnp.dot(a, b, preferred_element_type=F32)


def dot_t(a, b):
    return lax.dot_general(a, b, (((1,), (1,)), ((), ())), preferred_element_type=F32)


def iota(shape, dim):
    return lax.broadcasted_iota(I32, shape, dim)


def mask(cond):
    return jnp.where(cond, 1.0, 0.0).astype(BF)


def start_kernel(x_ref, dy_ref, ids_ref, gates_ref, msg_ref, all_ref):
    msg_ref[...] = jnp.zeros_like(msg_ref)
    all_ref[...] = jnp.zeros_like(all_ref)
    all_ref[0:OWN, 0:D] = x_ref[...]
    all_ref[0:OWN, D : 2 * D] = dy_ref[...]
    row = iota((6, META), 0)
    lane = iota((6, META), 1)
    place = [jnp.where(lane == row + 6 * i, 1.0, 0.0).astype(BF) for i in range(2)]
    cols = (((0,), (0,)), ((), ()))
    meta = lax.dot_general(
        ids_ref[...].astype(F32).astype(BF), place[0], cols, preferred_element_type=F32
    ) + lax.dot_general(gates_ref[...], place[1], cols, preferred_element_type=F32)
    meta = meta.astype(BF)
    for t in range(NT):
        src = x_ref if t < 4 else dy_ref
        low = FA + FB * (t % 4)
        msg_ref[t, 0:OWN, 0:FB] = src[:, low : low + FB]
        low = LA + LB * (t % 4)
        msg_ref[t, 0:OWN, FB : FB + LB] = src[:, low : low + LB]
        msg_ref[t, 0:OWN, FB + LB : FB + LB + META] = meta


def positions(meta):
    ids = meta.astype(F32).astype(I32)
    lane = iota((NTOK, 128), 1)
    row = iota((NTOK, 128), 0)
    hit = jnp.zeros((NTOK, 128), jnp.bool_)
    for k in range(6):
        hit = hit | ((ids[:, k : k + 1] >> 1) == (lane >> 1))
    member = jnp.where(hit & ((row & 15) < OWN), 1.0, 0.0)
    lower = jnp.where(lane < row, 1.0, 0.0).astype(BF)
    earlier = dot(lower, member.astype(BF))
    return jnp.where(member > 0.5, earlier, -1.0), ids


def one_hots(pos):
    row = iota((ROWS, 128), 0)
    lane = iota((ROWS, 128), 1)
    pick = jnp.where(lane == 2 * (row >> 3), 1.0, 0.0).astype(BF)
    spread = dot_t(pick, pos.astype(BF)).astype(I32)
    sub = row & 7
    main = jnp.where(spread == sub, 1.0, 0.0).astype(BF)
    left = jnp.where(spread == 8 + (sub >> 2), 1.0, 0.0).astype(BF)
    return main, left


def pack_b_kernel(msg_ref, out_ref):
    meta = msg_ref[:, FB + LB : FB + LB + META]
    pos, ids = positions(meta)
    main, left = one_hots(pos)
    out_ref[:, 0:FB] = dot(main, msg_ref[:, 0:FB]).astype(BF)
    row = iota((ROWS, 128), 0)
    sub = row & 7
    pick = mask(iota((ROWS, 128), 1) == 2 * (row >> 3))
    spread = dot_t(pick, pos.astype(BF)).astype(I32)
    tiles = dot(mask(spread == 8 + (sub >> 1)), msg_ref[:, FB : FB + LB])
    tile = jnp.where((sub & 1) == 0, tiles[:, 0:128], tiles[:, 128:256])
    gates = meta.astype(F32)
    lane = iota((NTOK, 128), 1)
    weight = jnp.zeros((NTOK, 128), F32)
    for k in range(6):
        weight = weight + jnp.where(ids[:, k : k + 1] == lane, gates[:, 6 + k : 7 + k], 0.0)
    row16 = iota((16, 128), 0)
    gate_of = jnp.zeros((16, 128), F32)
    for s in range(10):
        col = jnp.sum(jnp.where(pos == float(s), weight, 0.0), axis=0, keepdims=True)
        gate_of = jnp.where(row16 == s, col, gate_of)
    gate_of = jnp.concatenate([gate_of, jnp.zeros((112, 128), F32)], axis=0).astype(BF)
    pick = mask((iota((ROWS, 128), 1) == 2 * (row >> 3) + (sub & 1)) & ((sub >> 1) == 2))
    out_ref[:, FB : FB + 128] = jnp.where(sub < 4, tile, dot_t(pick, gate_of)).astype(BF)


def unpack_b_kernel(in_ref, out_ref, gate_out, gate_ref, sem):
    out_ref[0:ROWS, :] = in_ref[:, 0:FB]
    turn = perm(False)
    turned = [dot(turn, in_ref[256 * h : 256 * (h + 1), FB : FB + 128]) for h in range(2)]
    turned = jnp.concatenate([turned[h][32 * r : 32 * (r + 1)] for r in range(6) for h in range(2)], axis=0)
    for r in range(4):
        out_ref[ROWS : ROWS + 64, 128 * r : 128 * (r + 1)] = turned[64 * r : 64 * (r + 1)].astype(BF)
    spread = mask((iota((ROWS, 64), 0) >> 3) == iota((ROWS, 64), 1))
    wide = iota((ROWS, 128), 1)
    sub = iota((ROWS, 128), 0) & 7
    main = jnp.zeros((ROWS, 128), F32)
    rest = jnp.zeros((128, 128), F32)
    lane = iota((128, 128), 1)
    for e in range(2):
        own = turned[64 * (4 + e) : 64 * (5 + e)]
        both = jnp.where(wide == sub, dot(spread, own.astype(BF)), 0.0)
        main = jnp.where(wide == e, jnp.sum(both, axis=1, keepdims=True), main)
        column = jnp.concatenate([own[:, 8:9], own[:, 9:10]], axis=0)
        rest = jnp.where(lane == e, column, rest)
    gate_ref[0:ROWS, :] = main
    gate_ref[ROWS : ROWS + 128, :] = rest
    copy = pltpu.make_async_copy(gate_ref, gate_out, sem)
    copy.start()
    copy.wait()


def pack_a_kernel(msg_ref, x_in, out_ref, x_ref, sem):
    copy = pltpu.make_async_copy(x_in, x_ref, sem)
    copy.start()
    pos, _ = positions(msg_ref[:, FB + LB : FB + LB + META])
    main, left = one_hots(pos)
    sub4 = iota((ROWS, 128), 0) & 3
    copy.wait()
    for part in range(2):
        out_ref[:, part * FA : (part + 1) * FA] = dot(main, x_ref[:, part * D : part * D + FA]).astype(BF)
        for q in range(LA // 512):
            low = part * D + 512 * q
            spread = dot(left, x_ref[:, low : low + 512])
            out = spread[:, 0:128]
            for k in range(1, 4):
                out = jnp.where(sub4 == k, spread[:, 128 * k : 128 * (k + 1)], out)
            low = 2 * FA + 128 * (part * (LA // 512) + q)
            out_ref[:, low : low + 128] = out.astype(BF)


def perm(inverse):
    row = iota((256, 256), 0)
    col = iota((256, 256), 1)
    if inverse:
        row, col = col, row
    return mask(((col & 7) == (row >> 5)) & ((col >> 3) == (row & 31)))


def grads(gate_pre, up_pre, back_proj, gates):
    lane = iota(gate_pre.shape, 1)
    scaled = back_proj * jnp.where(lane < HID2 // 2, gates[0], gates[1])
    sig = 1.0 / (1.0 + jnp.exp(-gate_pre))
    up_grad = (scaled * gate_pre * sig).astype(BF)
    gate_grad = (scaled * up_pre * sig * (1.0 + gate_pre * (1.0 - sig))).astype(BF)
    return gate_grad, up_grad


def experts_kernel(
    a_in,
    b_in,
    gates_in,
    wg_in,
    wu_in,
    wd_in,
    rs_out,
    send_out,
    a_ref,
    b_ref,
    gates_ref,
    wg_ref,
    wu_ref,
    wd_ref,
    left_ref,
    z_ref,
    rs_ref,
    send_ref,
    sems,
    out_sems,
):
    started = []

    def fetch(src, dst, parts):
        copies = []
        for part in parts:
            copies.append(pltpu.make_async_copy(src.at[part], dst.at[part], sems.at[len(started)]))
            copies[-1].start()
            started.append(copies[-1])
        return copies

    def fetch_weights(low):
        part = (slice(None), slice(None), pl.ds(low, 512))
        return [
            copy
            for src, dst in ((wg_in, wg_ref), (wu_in, wu_ref), (wd_in, wd_ref))
            for copy in fetch(src, dst, [part])
        ]

    def arrive(copies):
        for copy in copies:
            copy.wait()

    every = slice(None)
    left_copies = fetch(
        a_in, a_ref, [(pl.ds(256 * h, 256), pl.ds(2 * FA, SENT_A - 2 * FA)) for h in range(2)]
    )
    main_copies = fetch(a_in, a_ref, [(every, pl.ds(FA * i, FA)) for i in range(2)]) + fetch_weights(0)
    b_copies = [
        fetch(b_in, b_ref, [pl.ds(GATHERED * u + 288 * i, 288) for u in (t, t + 4) for i in range(2)])
        + fetch_weights(FA + FB * t)
        for t in range(4)
    ]
    g_copies = fetch(gates_in, gates_ref, [pl.ds(0, ROWS + 128)])
    turn = perm(False)
    turn_back = perm(True)
    arrive(left_copies)
    for h in range(2):
        turned = dot(turn, a_ref[256 * h : 256 * (h + 1), 2 * FA : SENT_A]).astype(BF)
        for q in range(2 * LA // 512):
            base = (q // (LA // 512)) * D + 512 * (q % (LA // 512))
            for s in range(2):
                for k in range(4):
                    low = 64 * s + 32 * h
                    left_ref[low : low + 32, base + 128 * k : base + 128 * (k + 1)] = turned[
                        32 * (4 * s + k) : 32 * (4 * s + k + 1), 128 * q : 128 * (q + 1)
                    ]
    arrive(main_copies)

    def block(ref, low):
        return ref[:, :, low : low + 512].reshape(HID2, 512)

    def add_left(sums, low):
        rows = left_ref[:, low : low + 512]
        products = (
            dot_t(rows, block(wg_ref, low)),
            dot_t(rows, block(wu_ref, low)),
            dot_t(left_ref[:, D + low : D + low + 512], block(wd_ref, low)),
        )
        return [a + b for a, b in zip(sums, products)]

    left_sums = add_left([0.0] * 3, 0)
    gate_pre = dot_t(a_ref[:, 0:FA], block(wg_ref, 0))
    up_pre = dot_t(a_ref[:, 0:FA], block(wu_ref, 0))
    back_proj = dot_t(a_ref[:, FA : 2 * FA], block(wd_ref, 0))
    for t in range(4):
        arrive(b_copies[t])
        low = FA + FB * t
        x0, y0 = GATHERED * t, GATHERED * (t + 4)
        rows = b_ref[x0 : x0 + ROWS, :]
        gate_pre = gate_pre + dot_t(rows, block(wg_ref, low))
        up_pre = up_pre + dot_t(rows, block(wu_ref, low))
        back_proj = back_proj + dot_t(b_ref[y0 : y0 + ROWS, :], block(wd_ref, low))
        for base, start in ((0, x0), (D, y0)):
            low = base + LA + LB * t
            for s in range(2):
                left_ref[64 * s : 64 * s + 64, low : low + LB] = b_ref[
                    start + ROWS : start + GATHERED, LB * s : LB * (s + 1)
                ]
        if FA + FB * (t + 1) <= LA:
            left_sums = add_left(left_sums, FA + FB * t)
    arrive(g_copies)
    wg = wg_ref[...].reshape(HID2, D)
    wu = wu_ref[...].reshape(HID2, D)
    for low in range(LA, D, 512):
        left_sums = add_left(left_sums, low)
    gate_left, up_left = grads(
        *left_sums,
        (gates_ref[ROWS : ROWS + 128, 0:1], gates_ref[ROWS : ROWS + 128, 1:2]),
    )
    gate_grad, up_grad = grads(
        gate_pre, up_pre, back_proj, (gates_ref[0:ROWS, 0:1], gates_ref[0:ROWS, 1:2])
    )

    def part(low, width):
        cols = slice(low, low + width)
        return (
            dot(gate_grad, wg[:, cols]) + dot(up_grad, wu[:, cols]),
            dot(gate_left, wg[:, cols]) + dot(up_left, wu[:, cols]),
        )

    outs = []
    rests = []
    for q in range(RA // 512):
        sums, rest = part(512 * q, 512)
        send_ref[:, 512 * q : 512 * (q + 1)] = sums.astype(BF)
        rests.append(rest.astype(BF))
    for h in range(2):
        for s in range(2):
            for k in range(4):
                low = 256 * h + 32 * (4 * s + k)
                z_ref[low : low + 32, :] = rests[1][64 * s + 32 * h : 64 * s + 32 * h + 32, 128 * k : 128 * (k + 1)]
        rows = slice(256 * h, 256 * (h + 1))
        send_ref[rows, RA:BACK_A] = dot(turn_back, z_ref[rows, :]).astype(BF)
        for i in range(2 * h, 2 * h + 2):
            rows = pl.ds(128 * i, 128)
            outs.append(pltpu.make_async_copy(send_ref.at[rows], send_out.at[rows], out_sems.at[NT + i]))
            outs[-1].start()
    row = iota((256, 256), 0)
    col = iota((256, 256), 1)
    place_main = mask(((col >> 3) == (row >> 3)) & (((col & 7) >> 1) == (row & 7)))
    row = iota((ROWS, 256), 0)
    col = iota((ROWS, 256), 1)
    place_left = mask(((col & 63) == (row >> 3)) & ((row & 7) == 4 + (col >> 6)))

    def halves(tile, odd_rows, odd_slice):
        low_half = iota(tile.shape, 1) < 64
        moved = pltpu.roll(tile, 64, 1)
        both = jnp.where(low_half, moved, tile) if odd_slice else jnp.where(low_half, tile, moved)
        return jnp.where(low_half == odd_rows, 0.0, both).astype(BF)

    odd_main = (iota((ROWS, 128), 0) & 1) == 1
    odd_left = iota((128, 128), 0) >= 64
    for c in range(2):
        half_main, half_left = part(2048 + 256 * c, 256)
        for pair in range(2):
            t0 = 4 * c + 2 * pair
            full_main, full_left = part(RA + 128 * t0, 256)
            tile_main = half_main[:, 128 * pair : 128 * (pair + 1)]
            tile_left = half_left[:, 128 * pair : 128 * (pair + 1)]
            mains = jnp.concatenate([halves(tile_main, odd_main, i == 1) for i in range(2)], axis=1)
            halves_left = [halves(tile_left, odd_left, i == 1) for i in range(2)]
            extra = [
                rests[0][64 * (t // 4) : 64 * (t // 4) + 64, 128 * (t % 4) : 128 * (t % 4 + 1)]
                for t in (t0, t0 + 1)
            ]
            lefts = jnp.concatenate(
                [
                    full_left.astype(BF),
                    jnp.concatenate([half[0:64] + half[64:128] for half in halves_left], axis=1),
                    jnp.concatenate(extra, axis=1),
                ],
                axis=0,
            )
            placed = dot(place_left, lefts)
            for h in range(2):
                rows = slice(256 * h, 256 * (h + 1))
                both = (placed[rows] + dot(place_main, mains[rows])).astype(BF)
                for i in range(2):
                    rs_ref[t0 + i, rows, 128:256] = both[:, 128 * i : 128 * (i + 1)]
            for i in range(2):
                rs_ref[t0 + i, :, 0:128] = full_main[:, 128 * i : 128 * (i + 1)].astype(BF)
                outs.append(pltpu.make_async_copy(rs_ref.at[t0 + i], rs_out.at[t0 + i], out_sems.at[t0 + i]))
                outs[-1].start()
    for copy in outs:
        copy.wait()


def spread_positions(msg_ref):
    pos, _ = positions(msg_ref[:, FB + LB : FB + LB + META])
    row = iota((128, ROWS), 0)
    col = iota((128, ROWS), 1)
    pick = jnp.where(row == 2 * (col >> 3), 1.0, 0.0).astype(BF)
    return dot(pos.astype(BF), pick).astype(I32), col & 7


def combine_a_kernel(msg_ref, a_ref, out_ref):
    spread, sub = spread_positions(msg_ref)
    main = mask(spread == sub)
    total = dot(main, a_ref[:, 0:RA])
    out_ref[:, 0:512] = total[:, 0:512].astype(BF)
    for k in range(4):
        left = mask((spread == 8 + (sub >> 2)) & ((sub & 3) == k))
        low = 512 + 128 * k
        rest = dot(left, a_ref[:, RA:BACK_A])
        out_ref[:, low : low + 128] = (total[:, low : low + 128] + rest).astype(BF)


def combine_b_kernel(msg_ref, b_ref, a_ref, slice_ref, out_ref):
    spread, sub = spread_positions(msg_ref)
    main = mask(spread == sub)
    tile = b_ref[:, 128:256]
    rest = mask(((sub == 4) & (spread == 8)) | ((sub == 5) & (spread == 9)))
    full = dot(main, b_ref[:, 0:128]) + dot(rest, tile)
    low = dot(mask(((sub < 4) & (spread == 2 * sub)) | ((sub == 6) & (spread == 8))), tile)
    high = dot(mask(((sub < 4) & (spread == 2 * sub + 1)) | ((sub == 6) & (spread == 9))), tile)
    both = jnp.where(iota((NTOK, 128), 1) < 64, low, high)
    both = both + pltpu.roll(both, 64, 1)
    me = slice_ref[0, 0]
    extra = dot(mask((sub == 7) & (spread == 8 + (me >> 2))), tile)
    tiles = [
        a_ref[:, 128 * j : 128 * (j + 1)].astype(F32) + jnp.where((me & 3) == j, extra, 0.0)
        for j in range(4)
    ]
    tiles += [a_ref[:, 512:RA].astype(F32), full, both]
    values = jnp.concatenate([tile.astype(BF) for tile in tiles], axis=1)
    row = iota((64, NTOK), 0)
    col = iota((64, NTOK), 1)
    out_ref[:, 0:LAST] = dot(mask(col == 16 * (row >> 3) + (row & 7)), values).astype(BF)
    spread = [
        dot(mask((col == 16 * (row >> 3) + 8 + (row & 3)) & (((row >> 2) & 1) == i)), values)
        for i in range(2)
    ]
    for j in range(LAST // 256):
        packed = spread[0][:, 256 * j : 256 * j + 128] + spread[1][:, 256 * j + 128 : 256 * (j + 1)]
        out_ref[:, LAST + 128 * j : LAST + 128 * (j + 1)] = packed.astype(BF)


def finish_kernel(in_ref, out_ref):
    def tile(t, j):
        first = in_ref[t, :, 128 * j : 128 * (j + 1)].astype(F32)
        low = LAST + 128 * (j // 2)
        rest = in_ref[t, :, low : low + 128].astype(F32)
        return first, rest

    def store(low, first, rest, odd):
        rest = pltpu.roll(rest, 4, 0) if odd else rest
        out_ref[:, low : low + 128] = jnp.concatenate([first, rest], axis=0).astype(BF)[0:OWN]

    for j in range(RA // 128):
        first, rest = tile(0, j)
        for t in range(1, NT):
            more = tile(t, j)
            first, rest = first + more[0], rest + more[1]
        store(128 * j, first, rest, j % 2 == 1)
    for t in range(NT):
        store(RA + 128 * t, *tile(t, RA // 128), False)
    low_half = iota((8, 128), 1) < 64
    for t in range(0, NT, 2):
        pair = zip(tile(t, RA // 128 + 1), tile(t + 1, RA // 128 + 1))
        store(2048 + 64 * t, *[jnp.where(low_half, one, two) for one, two in pair], True)


def shape(*dims, dtype=BF):
    return jax.ShapeDtypeStruct(dims, dtype)


def per_device(tokens, out_grad, expert_ids, gate_values, gate_weight, up_weight, down_weight):
    weights = (gate_weight, up_weight, down_weight)
    lanes = FB + LB + META
    msg, both = call(start_kernel, (shape(NT, PADDED, lanes), shape(PADDED, 2 * D)), "start", limit=LARGE)(
        tokens, out_grad, expert_ids.T, gate_values.T
    )
    both_all = lax.all_gather(both, "tensor", axis=0, tiled=True)
    msg = lax.all_to_all(msg, "tensor", 0, 0, tiled=True).reshape(NTOK, lanes)
    send_b = call(pack_b_kernel, shape(ROWS, SENT_B), "pack_b", flops=2 * ROWS * 128 * 1280)(msg)
    recv_b = lax.all_to_all(send_b.reshape(NE, 8, SENT_B), "expert", 0, 0, tiled=True)
    own_b, gates = call(
        unpack_b_kernel,
        (shape(GATHERED, FB), shape(ROWS + 128, 128, dtype=F32)),
        "unpack_b",
        flops=2 * ROWS * ROWS * 128,
        scratch=[pltpu.VMEM((ROWS + 128, 128), F32), pltpu.SemaphoreType.DMA],
        outs=(VMEM, HBM),
    )(recv_b.reshape(ROWS, SENT_B))
    all_b = lax.all_gather(own_b, "tensor", axis=0, tiled=True)
    send_a = call(
        pack_a_kernel,
        shape(ROWS, SENT_A),
        "pack_a",
        flops=2 * ROWS * 128 * 4096,
        scratch=[pltpu.VMEM((NTOK, 2 * D), BF), pltpu.SemaphoreType.DMA],
        ins=[VMEM, HBM],
    )(msg, both_all)
    recv_a = lax.all_to_all(send_a.reshape(NE, 8, SENT_A), "expert", 0, 0, tiled=True)
    to_sum, to_send = call(
        experts_kernel,
        (shape(NT, ROWS, RB), shape(ROWS, BACK_A)),
        "experts",
        flops=10 * 640 * D * HID2,
        moved=13_000_000,
        scratch=[
            pltpu.VMEM((ROWS, SENT_A), BF),
            pltpu.VMEM((NT * GATHERED, FB), BF),
            pltpu.VMEM((ROWS + 128, 128), F32),
            pltpu.VMEM((2, HID2 // 2, D), BF),
            pltpu.VMEM((2, HID2 // 2, D), BF),
            pltpu.VMEM((2, HID2 // 2, D), BF),
            pltpu.VMEM((128, 2 * D), BF),
            pltpu.VMEM((ROWS, 128), BF),
            pltpu.VMEM((NT, ROWS, RB), BF),
            pltpu.VMEM((ROWS, BACK_A), BF),
            pltpu.SemaphoreType.DMA((36,)),
            pltpu.SemaphoreType.DMA((NT + 4,)),
        ],
        limit=LARGE,
        ins=[HBM] * 6,
        outs=(HBM, HBM),
    )(recv_a.reshape(ROWS, SENT_A), all_b, gates, *weights)
    summed = lax.psum_scatter(to_sum, "tensor", scatter_dimension=0, tiled=False)
    back_a = lax.all_to_all(to_send.reshape(NE, 8, BACK_A), "expert", 0, 0, tiled=True)
    back_b = lax.all_to_all(summed.reshape(NE, 8, RB), "expert", 0, 0, tiled=True)
    part_a = call(combine_a_kernel, shape(NTOK, RA), "combine_a", flops=2 * ROWS * 128 * 2048)(
        msg, back_a.reshape(ROWS, BACK_A)
    )
    me = lax.axis_index("tensor").astype(I32).reshape(1, 1)
    last = call(
        combine_b_kernel,
        shape(64, LAST_PACKED),
        "combine_b",
        flops=2 * ROWS * 128 * 1024,
        ins=[VMEM, VMEM, VMEM, pl.BlockSpec(memory_space=pltpu.SMEM)],
    )(msg, back_b.reshape(ROWS, RB), part_a, me)
    last = lax.all_to_all(last.reshape(NT, 8, LAST_PACKED), "tensor", 0, 0, tiled=True)
    return call(finish_kernel, shape(OWN, D), "finish")(last)


def solution(mesh):
    return jax.shard_map(
        per_device,
        mesh=mesh,
        in_specs=(
            P(("expert", "tensor"), None),
            P(("expert", "tensor"), None),
            P(("expert", "tensor"), None),
            P(("expert", "tensor"), None),
            P("expert", "tensor", None),
            P("expert", "tensor", None),
            P("expert", "tensor", None),
        ),
        out_specs=P(("expert", "tensor"), None),
        check_vma=False,
    )
```

```python
import jax
import jax.numpy as jnp
from jax import lax
from jax.experimental import pallas as pl
from jax.experimental.pallas import tpu as pltpu
from jax.sharding import PartitionSpec as P

BF = jnp.bfloat16
F32 = jnp.float32
I32 = jnp.int32
D = 2560
OWN = 12
PADDED = 16
NT = 8
NE = 64
NTOK = NT * PADDED
ROWS = NE * 8
HID2 = 192
FA = 512
FB = (D - FA) // 4
LA = 1536
LB = (D - LA) // 4
META = 128
SENT_A = 2 * FA + 2 * 2 * LA // 8
SENT_B = FB + 128
GATHERED = ROWS + NE
RA = 1024
RB = 256
BACK_A = RA + 128
LAST = RA + RB
LAST_PACKED = LAST * 3 // 2
SMALL = 24 * 1024 * 1024
LARGE = 60 * 1024 * 1024


HBM = pl.BlockSpec(memory_space=pltpu.HBM)
VMEM = pl.BlockSpec(memory_space=pltpu.VMEM)


def call(kernel, out_shapes, name, flops=0, moved=0, scratch=(), limit=SMALL, ins=None, outs=None):
    specs = {}
    if ins is not None:
        specs["in_specs"] = ins
    if outs is not None:
        specs["out_specs"] = outs
    return pl.pallas_call(
        kernel,
        out_shape=out_shapes,
        **specs,
        scratch_shapes=scratch,
        name=name,
        cost_estimate=pl.CostEstimate(flops=flops, bytes_accessed=moved, transcendentals=0),
        compiler_params=pltpu.CompilerParams(vmem_limit_bytes=limit),
    )


def dot(a, b):
    return jnp.dot(a, b, preferred_element_type=F32)


def dot_t(a, b):
    return lax.dot_general(a, b, (((1,), (1,)), ((), ())), preferred_element_type=F32)


def iota(shape, dim):
    return lax.broadcasted_iota(I32, shape, dim)


def mask(cond):
    return jnp.where(cond, 1.0, 0.0).astype(BF)


def start_kernel(x_ref, dy_ref, ids_ref, gates_ref, msg_ref, all_ref):
    msg_ref[...] = jnp.zeros_like(msg_ref)
    all_ref[...] = jnp.zeros_like(all_ref)
    all_ref[0:OWN, 0:D] = x_ref[...]
    all_ref[0:OWN, D : 2 * D] = dy_ref[...]
    row = iota((6, META), 0)
    lane = iota((6, META), 1)
    place = [jnp.where(lane == row + 6 * i, 1.0, 0.0).astype(BF) for i in range(2)]
    cols = (((0,), (0,)), ((), ()))
    meta = lax.dot_general(
        ids_ref[...].astype(F32).astype(BF), place[0], cols, preferred_element_type=F32
    ) + lax.dot_general(gates_ref[...], place[1], cols, preferred_element_type=F32)
    meta = meta.astype(BF)
    for t in range(NT):
        src = x_ref if t < 4 else dy_ref
        low = FA + FB * (t % 4)
        msg_ref[t, 0:OWN, 0:FB] = src[:, low : low + FB]
        low = LA + LB * (t % 4)
        msg_ref[t, 0:OWN, FB : FB + LB] = src[:, low : low + LB]
        msg_ref[t, 0:OWN, FB + LB : FB + LB + META] = meta


def positions(meta):
    ids = meta.astype(F32).astype(I32)
    lane = iota((NTOK, 128), 1)
    row = iota((NTOK, 128), 0)
    hit = jnp.zeros((NTOK, 128), jnp.bool_)
    for k in range(6):
        hit = hit | ((ids[:, k : k + 1] >> 1) == (lane >> 1))
    member = jnp.where(hit & ((row & 15) < OWN), 1.0, 0.0)
    lower = jnp.where(lane < row, 1.0, 0.0).astype(BF)
    earlier = dot(lower, member.astype(BF))
    return jnp.where(member > 0.5, earlier, -1.0), ids


def one_hots(pos):
    row = iota((ROWS, 128), 0)
    lane = iota((ROWS, 128), 1)
    pick = jnp.where(lane == 2 * (row >> 3), 1.0, 0.0).astype(BF)
    spread = dot_t(pick, pos.astype(BF)).astype(I32)
    sub = row & 7
    main = jnp.where(spread == sub, 1.0, 0.0).astype(BF)
    left = jnp.where(spread == 8 + (sub >> 2), 1.0, 0.0).astype(BF)
    return main, left


def pack_b_kernel(msg_ref, out_ref):
    meta = msg_ref[:, FB + LB : FB + LB + META]
    pos, ids = positions(meta)
    main, left = one_hots(pos)
    out_ref[:, 0:FB] = dot(main, msg_ref[:, 0:FB]).astype(BF)
    row = iota((ROWS, 128), 0)
    sub = row & 7
    pick = mask(iota((ROWS, 128), 1) == 2 * (row >> 3))
    spread = dot_t(pick, pos.astype(BF)).astype(I32)
    tiles = dot(mask(spread == 8 + (sub >> 1)), msg_ref[:, FB : FB + LB])
    tile = jnp.where((sub & 1) == 0, tiles[:, 0:128], tiles[:, 128:256])
    gates = meta.astype(F32)
    lane = iota((NTOK, 128), 1)
    weight = jnp.zeros((NTOK, 128), F32)
    for k in range(6):
        weight = weight + jnp.where(ids[:, k : k + 1] == lane, gates[:, 6 + k : 7 + k], 0.0)
    row16 = iota((16, 128), 0)
    gate_of = jnp.zeros((16, 128), F32)
    for s in range(10):
        col = jnp.sum(jnp.where(pos == float(s), weight, 0.0), axis=0, keepdims=True)
        gate_of = jnp.where(row16 == s, col, gate_of)
    gate_of = jnp.concatenate([gate_of, jnp.zeros((112, 128), F32)], axis=0).astype(BF)
    pick = mask((iota((ROWS, 128), 1) == 2 * (row >> 3) + (sub & 1)) & ((sub >> 1) == 2))
    out_ref[:, FB : FB + 128] = jnp.where(sub < 4, tile, dot_t(pick, gate_of)).astype(BF)


def unpack_b_kernel(in_ref, out_ref):
    out_ref[0:ROWS, :] = in_ref[:, 0:FB]
    turn = perm(False)[0:128]
    for h in range(2):
        turned = dot(turn, in_ref[256 * h : 256 * (h + 1), FB : FB + 128]).astype(BF)
        for r in range(4):
            low = ROWS + 32 * h
            out_ref[low : low + 32, 128 * r : 128 * (r + 1)] = turned[32 * r : 32 * (r + 1)]


def gates_as_columns(tile_ref, gate_ref):
    turn = perm(False)[128:192]
    turned = [dot(turn, tile_ref[256 * h : 256 * (h + 1), :]) for h in range(2)]
    spread = mask((iota((ROWS, 64), 0) >> 3) == iota((ROWS, 64), 1))
    wide = iota((ROWS, 128), 1)
    sub = iota((ROWS, 128), 0) & 7
    main = jnp.zeros((ROWS, 128), F32)
    rest = jnp.zeros((128, 128), F32)
    lane = iota((128, 128), 1)
    for e in range(2):
        own = jnp.concatenate([part[32 * e : 32 * (e + 1)] for part in turned], axis=0)
        both = jnp.where(wide == sub, dot(spread, own.astype(BF)), 0.0)
        main = jnp.where(wide == e, jnp.sum(both, axis=1, keepdims=True), main)
        column = jnp.concatenate([own[:, 8:9], own[:, 9:10]], axis=0)
        rest = jnp.where(lane == e, column, rest)
    gate_ref[0:ROWS, :] = main
    gate_ref[ROWS : ROWS + 128, :] = rest


def pack_a_kernel(msg_ref, tile_ref, x_in, out_ref, gate_ref, x_ref, sem):
    copy = pltpu.make_async_copy(x_in, x_ref, sem)
    copy.start()
    gates_as_columns(tile_ref, gate_ref)
    pos, _ = positions(msg_ref[:, FB + LB : FB + LB + META])
    main, left = one_hots(pos)
    sub4 = iota((ROWS, 128), 0) & 3
    copy.wait()
    for part in range(2):
        out_ref[:, part * FA : (part + 1) * FA] = dot(main, x_ref[:, part * D : part * D + FA]).astype(BF)
        for q in range(LA // 512):
            low = part * D + 512 * q
            spread = dot(left, x_ref[:, low : low + 512])
            out = spread[:, 0:128]
            for k in range(1, 4):
                out = jnp.where(sub4 == k, spread[:, 128 * k : 128 * (k + 1)], out)
            low = 2 * FA + 128 * (part * (LA // 512) + q)
            out_ref[:, low : low + 128] = out.astype(BF)


def perm(inverse):
    row = iota((256, 256), 0)
    col = iota((256, 256), 1)
    if inverse:
        row, col = col, row
    return mask(((col & 7) == (row >> 5)) & ((col >> 3) == (row & 31)))


def grads(gate_pre, up_pre, back_proj, gates):
    lane = iota(gate_pre.shape, 1)
    scaled = back_proj * jnp.where(lane < HID2 // 2, gates[0], gates[1])
    sig = 1.0 / (1.0 + jnp.exp(-gate_pre))
    up_grad = (scaled * gate_pre * sig).astype(BF)
    gate_grad = (scaled * up_pre * sig * (1.0 + gate_pre * (1.0 - sig))).astype(BF)
    return gate_grad, up_grad


def experts_kernel(
    a_in,
    b_in,
    gates_in,
    wg_in,
    wu_in,
    wd_in,
    rs_out,
    send_out,
    a_ref,
    b_ref,
    gates_ref,
    wg_ref,
    wu_ref,
    wd_ref,
    left_ref,
    z_ref,
    rs_ref,
    send_ref,
    sems,
    out_sems,
):
    started = []

    def fetch(src, dst, parts):
        copies = []
        for part in parts:
            copies.append(pltpu.make_async_copy(src.at[part], dst.at[part], sems.at[len(started)]))
            copies[-1].start()
            started.append(copies[-1])
        return copies

    def fetch_weights(low):
        part = (slice(None), slice(None), pl.ds(low, 512))
        return [
            copy
            for src, dst in ((wg_in, wg_ref), (wu_in, wu_ref), (wd_in, wd_ref))
            for copy in fetch(src, dst, [part])
        ]

    def arrive(copies):
        for copy in copies:
            copy.wait()

    every = slice(None)
    left_copies = fetch(
        a_in, a_ref, [(pl.ds(256 * h, 256), pl.ds(2 * FA, SENT_A - 2 * FA)) for h in range(2)]
    )
    main_copies = fetch(a_in, a_ref, [(every, pl.ds(FA * i, FA)) for i in range(2)]) + fetch_weights(0)
    b_copies = [
        fetch(b_in, b_ref, [pl.ds(GATHERED * u + 288 * i, 288) for u in (t, t + 4) for i in range(2)])
        + fetch_weights(FA + FB * t)
        for t in range(4)
    ]
    g_copies = fetch(gates_in, gates_ref, [pl.ds(0, ROWS + 128)])
    turn = perm(False)
    turn_back = perm(True)
    arrive(left_copies)
    for h in range(2):
        turned = dot(turn, a_ref[256 * h : 256 * (h + 1), 2 * FA : SENT_A]).astype(BF)
        for q in range(2 * LA // 512):
            base = (q // (LA // 512)) * D + 512 * (q % (LA // 512))
            for s in range(2):
                for k in range(4):
                    low = 64 * s + 32 * h
                    left_ref[low : low + 32, base + 128 * k : base + 128 * (k + 1)] = turned[
                        32 * (4 * s + k) : 32 * (4 * s + k + 1), 128 * q : 128 * (q + 1)
                    ]
    arrive(main_copies)

    def block(ref, low):
        return ref[:, :, low : low + 512].reshape(HID2, 512)

    def add_left(sums, low):
        rows = left_ref[:, low : low + 512]
        products = (
            dot_t(rows, block(wg_ref, low)),
            dot_t(rows, block(wu_ref, low)),
            dot_t(left_ref[:, D + low : D + low + 512], block(wd_ref, low)),
        )
        return [a + b for a, b in zip(sums, products)]

    left_sums = add_left([0.0] * 3, 0)
    gate_pre = dot_t(a_ref[:, 0:FA], block(wg_ref, 0))
    up_pre = dot_t(a_ref[:, 0:FA], block(wu_ref, 0))
    back_proj = dot_t(a_ref[:, FA : 2 * FA], block(wd_ref, 0))
    for t in range(4):
        arrive(b_copies[t])
        low = FA + FB * t
        x0, y0 = GATHERED * t, GATHERED * (t + 4)
        rows = b_ref[x0 : x0 + ROWS, :]
        gate_pre = gate_pre + dot_t(rows, block(wg_ref, low))
        up_pre = up_pre + dot_t(rows, block(wu_ref, low))
        back_proj = back_proj + dot_t(b_ref[y0 : y0 + ROWS, :], block(wd_ref, low))
        for base, start in ((0, x0), (D, y0)):
            low = base + LA + LB * t
            for s in range(2):
                left_ref[64 * s : 64 * s + 64, low : low + LB] = b_ref[
                    start + ROWS : start + GATHERED, LB * s : LB * (s + 1)
                ]
        if FA + FB * (t + 1) <= LA:
            left_sums = add_left(left_sums, FA + FB * t)
    arrive(g_copies)
    wg = wg_ref[...].reshape(HID2, D)
    wu = wu_ref[...].reshape(HID2, D)
    for low in range(LA, D, 512):
        left_sums = add_left(left_sums, low)
    gate_left, up_left = grads(
        *left_sums,
        (gates_ref[ROWS : ROWS + 128, 0:1], gates_ref[ROWS : ROWS + 128, 1:2]),
    )
    gate_grad, up_grad = grads(
        gate_pre, up_pre, back_proj, (gates_ref[0:ROWS, 0:1], gates_ref[0:ROWS, 1:2])
    )

    def part(low, width):
        cols = slice(low, low + width)
        return (
            dot(gate_grad, wg[:, cols]) + dot(up_grad, wu[:, cols]),
            dot(gate_left, wg[:, cols]) + dot(up_left, wu[:, cols]),
        )

    outs = []
    rests = []
    for q in range(RA // 512):
        sums, rest = part(512 * q, 512)
        send_ref[:, 512 * q : 512 * (q + 1)] = sums.astype(BF)
        rests.append(rest.astype(BF))
    for h in range(2):
        for s in range(2):
            for k in range(4):
                low = 256 * h + 32 * (4 * s + k)
                z_ref[low : low + 32, :] = rests[1][64 * s + 32 * h : 64 * s + 32 * h + 32, 128 * k : 128 * (k + 1)]
        rows = slice(256 * h, 256 * (h + 1))
        send_ref[rows, RA:BACK_A] = dot(turn_back, z_ref[rows, :]).astype(BF)
        for i in range(2 * h, 2 * h + 2):
            rows = pl.ds(128 * i, 128)
            outs.append(pltpu.make_async_copy(send_ref.at[rows], send_out.at[rows], out_sems.at[NT + i]))
            outs[-1].start()
    row = iota((256, 256), 0)
    col = iota((256, 256), 1)
    place_main = mask(((col >> 3) == (row >> 3)) & (((col & 7) >> 1) == (row & 7)))
    row = iota((ROWS, 256), 0)
    col = iota((ROWS, 256), 1)
    place_left = mask(((col & 63) == (row >> 3)) & ((row & 7) == 4 + (col >> 6)))

    def halves(tile, odd_rows, odd_slice):
        low_half = iota(tile.shape, 1) < 64
        moved = pltpu.roll(tile, 64, 1)
        both = jnp.where(low_half, moved, tile) if odd_slice else jnp.where(low_half, tile, moved)
        return jnp.where(low_half == odd_rows, 0.0, both).astype(BF)

    odd_main = (iota((ROWS, 128), 0) & 1) == 1
    odd_left = iota((128, 128), 0) >= 64
    for c in range(2):
        half_main, half_left = part(2048 + 256 * c, 256)
        for pair in range(2):
            t0 = 4 * c + 2 * pair
            full_main, full_left = part(RA + 128 * t0, 256)
            tile_main = half_main[:, 128 * pair : 128 * (pair + 1)]
            tile_left = half_left[:, 128 * pair : 128 * (pair + 1)]
            mains = jnp.concatenate([halves(tile_main, odd_main, i == 1) for i in range(2)], axis=1)
            halves_left = [halves(tile_left, odd_left, i == 1) for i in range(2)]
            extra = [
                rests[0][64 * (t // 4) : 64 * (t // 4) + 64, 128 * (t % 4) : 128 * (t % 4 + 1)]
                for t in (t0, t0 + 1)
            ]
            lefts = jnp.concatenate(
                [
                    full_left.astype(BF),
                    jnp.concatenate([half[0:64] + half[64:128] for half in halves_left], axis=1),
                    jnp.concatenate(extra, axis=1),
                ],
                axis=0,
            )
            placed = dot(place_left, lefts)
            for h in range(2):
                rows = slice(256 * h, 256 * (h + 1))
                both = (placed[rows] + dot(place_main, mains[rows])).astype(BF)
                for i in range(2):
                    rs_ref[t0 + i, rows, 128:256] = both[:, 128 * i : 128 * (i + 1)]
            for i in range(2):
                rs_ref[t0 + i, :, 0:128] = full_main[:, 128 * i : 128 * (i + 1)].astype(BF)
                outs.append(pltpu.make_async_copy(rs_ref.at[t0 + i], rs_out.at[t0 + i], out_sems.at[t0 + i]))
                outs[-1].start()
    for copy in outs:
        copy.wait()


def spread_positions(msg_ref):
    pos, _ = positions(msg_ref[:, FB + LB : FB + LB + META])
    row = iota((128, ROWS), 0)
    col = iota((128, ROWS), 1)
    pick = jnp.where(row == 2 * (col >> 3), 1.0, 0.0).astype(BF)
    return dot(pos.astype(BF), pick).astype(I32), col & 7


def combine_a_kernel(msg_ref, a_ref, out_ref):
    spread, sub = spread_positions(msg_ref)
    main = mask(spread == sub)
    total = dot(main, a_ref[:, 0:RA])
    out_ref[:, 0:512] = total[:, 0:512].astype(BF)
    for k in range(4):
        left = mask((spread == 8 + (sub >> 2)) & ((sub & 3) == k))
        low = 512 + 128 * k
        rest = dot(left, a_ref[:, RA:BACK_A])
        out_ref[:, low : low + 128] = (total[:, low : low + 128] + rest).astype(BF)


def combine_b_kernel(msg_ref, b_ref, a_ref, slice_ref, out_ref):
    spread, sub = spread_positions(msg_ref)
    main = mask(spread == sub)
    tile = b_ref[:, 128:256]
    rest = mask(((sub == 4) & (spread == 8)) | ((sub == 5) & (spread == 9)))
    full = dot(main, b_ref[:, 0:128]) + dot(rest, tile)
    low = dot(mask(((sub < 4) & (spread == 2 * sub)) | ((sub == 6) & (spread == 8))), tile)
    high = dot(mask(((sub < 4) & (spread == 2 * sub + 1)) | ((sub == 6) & (spread == 9))), tile)
    both = jnp.where(iota((NTOK, 128), 1) < 64, low, high)
    both = both + pltpu.roll(both, 64, 1)
    me = slice_ref[0, 0]
    extra = dot(mask((sub == 7) & (spread == 8 + (me >> 2))), tile)
    tiles = [
        a_ref[:, 128 * j : 128 * (j + 1)].astype(F32) + jnp.where((me & 3) == j, extra, 0.0)
        for j in range(4)
    ]
    tiles += [a_ref[:, 512:RA].astype(F32), full, both]
    values = jnp.concatenate([tile.astype(BF) for tile in tiles], axis=1)
    row = iota((64, NTOK), 0)
    col = iota((64, NTOK), 1)
    out_ref[:, 0:LAST] = dot(mask(col == 16 * (row >> 3) + (row & 7)), values).astype(BF)
    spread = [
        dot(mask((col == 16 * (row >> 3) + 8 + (row & 3)) & (((row >> 2) & 1) == i)), values)
        for i in range(2)
    ]
    for j in range(LAST // 256):
        packed = spread[0][:, 256 * j : 256 * j + 128] + spread[1][:, 256 * j + 128 : 256 * (j + 1)]
        out_ref[:, LAST + 128 * j : LAST + 128 * (j + 1)] = packed.astype(BF)


def finish_kernel(in_ref, out_ref):
    def tile(t, j):
        first = in_ref[t, :, 128 * j : 128 * (j + 1)].astype(F32)
        low = LAST + 128 * (j // 2)
        rest = in_ref[t, :, low : low + 128].astype(F32)
        return first, rest

    def store(low, first, rest, odd):
        rest = pltpu.roll(rest, 4, 0) if odd else rest
        out_ref[:, low : low + 128] = jnp.concatenate([first, rest], axis=0).astype(BF)[0:OWN]

    for j in range(RA // 128):
        first, rest = tile(0, j)
        for t in range(1, NT):
            more = tile(t, j)
            first, rest = first + more[0], rest + more[1]
        store(128 * j, first, rest, j % 2 == 1)
    for t in range(NT):
        store(RA + 128 * t, *tile(t, RA // 128), False)
    low_half = iota((8, 128), 1) < 64
    for t in range(0, NT, 2):
        pair = zip(tile(t, RA // 128 + 1), tile(t + 1, RA // 128 + 1))
        store(2048 + 64 * t, *[jnp.where(low_half, one, two) for one, two in pair], True)


def shape(*dims, dtype=BF):
    return jax.ShapeDtypeStruct(dims, dtype)


def per_device(tokens, out_grad, expert_ids, gate_values, gate_weight, up_weight, down_weight):
    weights = (gate_weight, up_weight, down_weight)
    lanes = FB + LB + META
    msg, both = call(start_kernel, (shape(NT, PADDED, lanes), shape(PADDED, 2 * D)), "start", limit=LARGE)(
        tokens, out_grad, expert_ids.T, gate_values.T
    )
    both_all = lax.all_gather(both, "tensor", axis=0, tiled=True)
    msg = lax.all_to_all(msg, "tensor", 0, 0, tiled=True).reshape(NTOK, lanes)
    send_b = call(pack_b_kernel, shape(ROWS, SENT_B), "pack_b", flops=2 * ROWS * 128 * 1280)(msg)
    recv_b = lax.all_to_all(send_b.reshape(NE, 8, SENT_B), "expert", 0, 0, tiled=True)
    recv_b = recv_b.reshape(ROWS, SENT_B)
    own_b = call(unpack_b_kernel, shape(GATHERED, FB), "unpack_b", flops=2 * ROWS * 256 * 128)(recv_b)
    all_b = lax.all_gather(own_b, "tensor", axis=0, tiled=True)
    send_a, gates = call(
        pack_a_kernel,
        (shape(ROWS, SENT_A), shape(ROWS + 128, 128, dtype=F32)),
        "pack_a",
        flops=2 * ROWS * 128 * 4096,
        scratch=[pltpu.VMEM((NTOK, 2 * D), BF), pltpu.SemaphoreType.DMA],
        ins=[VMEM, VMEM, HBM],
    )(msg, recv_b[:, FB:SENT_B], both_all)
    recv_a = lax.all_to_all(send_a.reshape(NE, 8, SENT_A), "expert", 0, 0, tiled=True)
    to_sum, to_send = call(
        experts_kernel,
        (shape(NT, ROWS, RB), shape(ROWS, BACK_A)),
        "experts",
        flops=10 * 640 * D * HID2,
        moved=13_000_000,
        scratch=[
            pltpu.VMEM((ROWS, SENT_A), BF),
            pltpu.VMEM((NT * GATHERED, FB), BF),
            pltpu.VMEM((ROWS + 128, 128), F32),
            pltpu.VMEM((2, HID2 // 2, D), BF),
            pltpu.VMEM((2, HID2 // 2, D), BF),
            pltpu.VMEM((2, HID2 // 2, D), BF),
            pltpu.VMEM((128, 2 * D), BF),
            pltpu.VMEM((ROWS, 128), BF),
            pltpu.VMEM((NT, ROWS, RB), BF),
            pltpu.VMEM((ROWS, BACK_A), BF),
            pltpu.SemaphoreType.DMA((36,)),
            pltpu.SemaphoreType.DMA((NT + 4,)),
        ],
        limit=LARGE,
        ins=[HBM] * 6,
        outs=(HBM, HBM),
    )(recv_a.reshape(ROWS, SENT_A), all_b, gates, *weights)
    summed = lax.psum_scatter(to_sum, "tensor", scatter_dimension=0, tiled=False)
    back_a = lax.all_to_all(to_send.reshape(NE, 8, BACK_A), "expert", 0, 0, tiled=True)
    back_b = lax.all_to_all(summed.reshape(NE, 8, RB), "expert", 0, 0, tiled=True)
    part_a = call(combine_a_kernel, shape(NTOK, RA), "combine_a", flops=2 * ROWS * 128 * 2048)(
        msg, back_a.reshape(ROWS, BACK_A)
    )
    me = lax.axis_index("tensor").astype(I32).reshape(1, 1)
    last = call(
        combine_b_kernel,
        shape(64, LAST_PACKED),
        "combine_b",
        flops=2 * ROWS * 128 * 1024,
        ins=[VMEM, VMEM, VMEM, pl.BlockSpec(memory_space=pltpu.SMEM)],
    )(msg, back_b.reshape(ROWS, RB), part_a, me)
    last = lax.all_to_all(last.reshape(NT, 8, LAST_PACKED), "tensor", 0, 0, tiled=True)
    return call(finish_kernel, shape(OWN, D), "finish")(last)


def solution(mesh):
    return jax.shard_map(
        per_device,
        mesh=mesh,
        in_specs=(
            P(("expert", "tensor"), None),
            P(("expert", "tensor"), None),
            P(("expert", "tensor"), None),
            P(("expert", "tensor"), None),
            P("expert", "tensor", None),
            P("expert", "tensor", None),
            P("expert", "tensor", None),
        ),
        out_specs=P(("expert", "tensor"), None),
        check_vma=False,
    )
```

```python
import jax
import jax.numpy as jnp
from jax import lax
from jax.experimental import pallas as pl
from jax.experimental.pallas import tpu as pltpu
from jax.sharding import PartitionSpec as P

BF = jnp.bfloat16
F32 = jnp.float32
I32 = jnp.int32
D = 2560
OWN = 12
PADDED = 16
NT = 8
NE = 64
NTOK = NT * PADDED
ROWS = NE * 8
HID2 = 192
FA = 512
FB = (D - FA) // 4
LA = 1536
LB = (D - LA) // 4
FOURTH = [D * (t // 4) + LA + LB * (t % 4) + 128 for t in range(8)]
META = 128
SENT_A = 2 * FA + 2 * 2 * LA // 8 + 128
SENT_B = FB + 128
GATHERED = ROWS + 48
RA = 1024
RB = 256
BACK_A = RA + 128
LAST = RA + RB
LAST_PACKED = LAST * 3 // 2
SMALL = 24 * 1024 * 1024
LARGE = 60 * 1024 * 1024


HBM = pl.BlockSpec(memory_space=pltpu.HBM)
VMEM = pl.BlockSpec(memory_space=pltpu.VMEM)


def call(kernel, out_shapes, name, flops=0, moved=0, scratch=(), limit=SMALL, ins=None, outs=None):
    specs = {}
    if ins is not None:
        specs["in_specs"] = ins
    if outs is not None:
        specs["out_specs"] = outs
    return pl.pallas_call(
        kernel,
        out_shape=out_shapes,
        **specs,
        scratch_shapes=scratch,
        name=name,
        cost_estimate=pl.CostEstimate(flops=flops, bytes_accessed=moved, transcendentals=0),
        compiler_params=pltpu.CompilerParams(vmem_limit_bytes=limit),
    )


def dot(a, b):
    return jnp.dot(a, b, preferred_element_type=F32)


def dot_t(a, b):
    return lax.dot_general(a, b, (((1,), (1,)), ((), ())), preferred_element_type=F32)


def iota(shape, dim):
    return lax.broadcasted_iota(I32, shape, dim)


def mask(cond):
    return jnp.where(cond, 1.0, 0.0).astype(BF)


def start_kernel(x_ref, dy_ref, ids_ref, gates_ref, msg_ref, all_ref):
    msg_ref[...] = jnp.zeros_like(msg_ref)
    all_ref[...] = jnp.zeros_like(all_ref)
    all_ref[0:OWN, 0:D] = x_ref[...]
    all_ref[0:OWN, D : 2 * D] = dy_ref[...]
    row = iota((6, META), 0)
    lane = iota((6, META), 1)
    place = [jnp.where(lane == row + 6 * i, 1.0, 0.0).astype(BF) for i in range(2)]
    cols = (((0,), (0,)), ((), ()))
    meta = lax.dot_general(
        ids_ref[...].astype(F32).astype(BF), place[0], cols, preferred_element_type=F32
    ) + lax.dot_general(gates_ref[...], place[1], cols, preferred_element_type=F32)
    meta = meta.astype(BF)
    for t in range(NT):
        src = x_ref if t < 4 else dy_ref
        low = FA + FB * (t % 4)
        msg_ref[t, 0:OWN, 0:FB] = src[:, low : low + FB]
        low = LA + LB * (t % 4)
        msg_ref[t, 0:OWN, FB : FB + LB] = src[:, low : low + LB]
        msg_ref[t, 0:OWN, FB + LB : FB + LB + META] = meta


def positions(meta):
    ids = meta.astype(F32).astype(I32)
    lane = iota((NTOK, 128), 1)
    row = iota((NTOK, 128), 0)
    hit = jnp.zeros((NTOK, 128), jnp.bool_)
    for k in range(6):
        hit = hit | ((ids[:, k : k + 1] >> 1) == (lane >> 1))
    member = jnp.where(hit & ((row & 15) < OWN), 1.0, 0.0)
    lower = jnp.where(lane < row, 1.0, 0.0).astype(BF)
    earlier = dot(lower, member.astype(BF))
    return jnp.where(member > 0.5, earlier, -1.0), ids


def one_hots(pos):
    row = iota((ROWS, 128), 0)
    lane = iota((ROWS, 128), 1)
    pick = jnp.where(lane == 2 * (row >> 3), 1.0, 0.0).astype(BF)
    spread = dot_t(pick, pos.astype(BF)).astype(I32)
    sub = row & 7
    main = jnp.where(spread == sub, 1.0, 0.0).astype(BF)
    left = jnp.where(spread == 8 + (sub >> 2), 1.0, 0.0).astype(BF)
    return main, left, mask(spread == 9)


def pack_b_kernel(msg_ref, out_ref):
    meta = msg_ref[:, FB + LB : FB + LB + META]
    pos, ids = positions(meta)
    main, left, _ = one_hots(pos)
    out_ref[:, 0:FB] = dot(main, msg_ref[:, 0:FB]).astype(BF)
    row = iota((ROWS, 128), 0)
    sub = row & 7
    pick = mask(iota((ROWS, 128), 1) == 2 * (row >> 3))
    spread = dot_t(pick, pos.astype(BF)).astype(I32)
    tiles = dot(mask(spread == 8 + (sub >> 1)), msg_ref[:, FB : FB + LB])
    tile = jnp.where((sub & 1) == 0, tiles[:, 0:128], tiles[:, 128:256])
    gates = meta.astype(F32)
    lane = iota((NTOK, 128), 1)
    weight = jnp.zeros((NTOK, 128), F32)
    for k in range(6):
        weight = weight + jnp.where(ids[:, k : k + 1] == lane, gates[:, 6 + k : 7 + k], 0.0)
    row16 = iota((16, 128), 0)
    gate_of = jnp.zeros((16, 128), F32)
    for s in range(10):
        col = jnp.sum(jnp.where(pos == float(s), weight, 0.0), axis=0, keepdims=True)
        gate_of = jnp.where(row16 == s, col, gate_of)
    gate_of = jnp.concatenate([gate_of, jnp.zeros((112, 128), F32)], axis=0).astype(BF)
    pick = mask((iota((ROWS, 128), 1) == 2 * (row >> 3) + (sub & 1)) & ((sub >> 1) == 2))
    out_ref[:, FB : FB + 128] = jnp.where(sub < 4, tile, dot_t(pick, gate_of)).astype(BF)


def unpack_b_kernel(in_ref, out_ref):
    out_ref[0:ROWS, :] = in_ref[:, 0:FB]
    turn = perm(False)[0:96]
    for h in range(2):
        turned = dot(turn, in_ref[256 * h : 256 * (h + 1), FB : FB + 128]).astype(BF)
        for r in range(3):
            for j in range(2):
                place = 64 * r + 32 * h + 16 * j
                low, tile = ROWS + place % 48, place // 48
                out_ref[low : low + 16, 128 * tile : 128 * (tile + 1)] = turned[
                    32 * r + 16 * j : 32 * r + 16 * (j + 1)
                ]


def gates_as_columns(tile_ref, gate_ref):
    turn = perm(False)[128:192]
    turned = [dot(turn, tile_ref[256 * h : 256 * (h + 1), :]) for h in range(2)]
    spread = mask((iota((ROWS, 64), 0) >> 3) == iota((ROWS, 64), 1))
    wide = iota((ROWS, 128), 1)
    sub = iota((ROWS, 128), 0) & 7
    main = jnp.zeros((ROWS, 128), F32)
    rest = jnp.zeros((128, 128), F32)
    lane = iota((128, 128), 1)
    for e in range(2):
        own = jnp.concatenate([part[32 * e : 32 * (e + 1)] for part in turned], axis=0)
        both = jnp.where(wide == sub, dot(spread, own.astype(BF)), 0.0)
        main = jnp.where(wide == e, jnp.sum(both, axis=1, keepdims=True), main)
        column = jnp.concatenate([own[:, 8:9], own[:, 9:10]], axis=0)
        rest = jnp.where(lane == e, column, rest)
    gate_ref[0:ROWS, :] = main
    gate_ref[ROWS : ROWS + 128, :] = rest


def pack_a_kernel(msg_ref, tile_ref, x_in, out_ref, gate_ref, x_ref, sem):
    copy = pltpu.make_async_copy(x_in, x_ref, sem)
    copy.start()
    gates_as_columns(tile_ref, gate_ref)
    pos, _ = positions(msg_ref[:, FB + LB : FB + LB + META])
    main, left, last = one_hots(pos)
    sub4 = iota((ROWS, 128), 0) & 3
    copy.wait()
    for part in range(2):
        out_ref[:, part * FA : (part + 1) * FA] = dot(main, x_ref[:, part * D : part * D + FA]).astype(BF)
        for q in range(LA // 512):
            low = part * D + 512 * q
            spread = dot(left, x_ref[:, low : low + 512])
            out = spread[:, 0:128]
            for k in range(1, 4):
                out = jnp.where(sub4 == k, spread[:, 128 * k : 128 * (k + 1)], out)
            low = 2 * FA + 128 * (part * (LA // 512) + q)
            out_ref[:, low : low + 128] = out.astype(BF)
    sub = iota((ROWS, 128), 0) & 7
    out = jnp.zeros((ROWS, 128), F32)
    for r in range(8):
        low = FOURTH[r]
        out = jnp.where(sub == r, dot(last, x_ref[:, low : low + 128]), out)
    out_ref[:, SENT_A - 128 : SENT_A] = out.astype(BF)


def perm(inverse):
    row = iota((256, 256), 0)
    col = iota((256, 256), 1)
    if inverse:
        row, col = col, row
    return mask(((col & 7) == (row >> 5)) & ((col >> 3) == (row & 31)))


def grads(gate_pre, up_pre, back_proj, gates):
    lane = iota(gate_pre.shape, 1)
    scaled = back_proj * jnp.where(lane < HID2 // 2, gates[0], gates[1])
    sig = 1.0 / (1.0 + jnp.exp(-gate_pre))
    up_grad = (scaled * gate_pre * sig).astype(BF)
    gate_grad = (scaled * up_pre * sig * (1.0 + gate_pre * (1.0 - sig))).astype(BF)
    return gate_grad, up_grad


def experts_kernel(
    a_in,
    b_in,
    gates_in,
    wg_in,
    wu_in,
    wd_in,
    rs_out,
    send_out,
    a_ref,
    b_ref,
    gates_ref,
    wg_ref,
    wu_ref,
    wd_ref,
    left_ref,
    z_ref,
    rs_ref,
    send_ref,
    sems,
    out_sems,
):
    started = []

    def fetch(src, dst, parts):
        copies = []
        for part in parts:
            copies.append(pltpu.make_async_copy(src.at[part], dst.at[part], sems.at[len(started)]))
            copies[-1].start()
            started.append(copies[-1])
        return copies

    def fetch_weights(low):
        part = (slice(None), slice(None), pl.ds(low, 512))
        return [
            copy
            for src, dst in ((wg_in, wg_ref), (wu_in, wu_ref), (wd_in, wd_ref))
            for copy in fetch(src, dst, [part])
        ]

    def arrive(copies):
        for copy in copies:
            copy.wait()

    every = slice(None)
    left_copies = fetch(
        a_in, a_ref, [(pl.ds(256 * h, 256), pl.ds(2 * FA, SENT_A - 2 * FA)) for h in range(2)]
    )
    main_copies = fetch(a_in, a_ref, [(every, pl.ds(FA * i, FA)) for i in range(2)]) + fetch_weights(0)
    b_copies = [
        fetch(b_in, b_ref, [pl.ds(GATHERED * u + 272 * i, 272 + 16 * i) for u in (t, t + 4) for i in range(2)])
        + fetch_weights(FA + FB * t)
        for t in range(4)
    ]
    g_copies = fetch(gates_in, gates_ref, [pl.ds(0, ROWS + 128)])
    turn = perm(False)
    turn_back = perm(True)
    arrive(left_copies)
    for h in range(2):
        turned = dot(turn, a_ref[256 * h : 256 * (h + 1), 2 * FA : SENT_A]).astype(BF)
        for q in range(2 * LA // 512):
            base = (q // (LA // 512)) * D + 512 * (q % (LA // 512))
            for s in range(2):
                for k in range(4):
                    low = 64 * s + 32 * h
                    left_ref[low : low + 32, base + 128 * k : base + 128 * (k + 1)] = turned[
                        32 * (4 * s + k) : 32 * (4 * s + k + 1), 128 * q : 128 * (q + 1)
                    ]
        for r in range(8):
            low = 64 + 32 * h
            left_ref[low : low + 32, FOURTH[r] : FOURTH[r] + 128] = turned[
                32 * r : 32 * (r + 1), 4 * LA // 8 : 4 * LA // 8 + 128
            ]
    arrive(main_copies)

    def block(ref, low):
        return ref[:, :, low : low + 512].reshape(HID2, 512)

    def add_left(sums, low):
        rows = left_ref[:, low : low + 512]
        products = (
            dot_t(rows, block(wg_ref, low)),
            dot_t(rows, block(wu_ref, low)),
            dot_t(left_ref[:, D + low : D + low + 512], block(wd_ref, low)),
        )
        return [a + b for a, b in zip(sums, products)]

    left_sums = add_left([0.0] * 3, 0)
    gate_pre = dot_t(a_ref[:, 0:FA], block(wg_ref, 0))
    up_pre = dot_t(a_ref[:, 0:FA], block(wu_ref, 0))
    back_proj = dot_t(a_ref[:, FA : 2 * FA], block(wd_ref, 0))
    for t in range(4):
        arrive(b_copies[t])
        low = FA + FB * t
        x0, y0 = GATHERED * t, GATHERED * (t + 4)
        rows = b_ref[x0 : x0 + ROWS, :]
        gate_pre = gate_pre + dot_t(rows, block(wg_ref, low))
        up_pre = up_pre + dot_t(rows, block(wu_ref, low))
        back_proj = back_proj + dot_t(b_ref[y0 : y0 + ROWS, :], block(wd_ref, low))
        for base, start in ((0, x0), (D, y0)):
            low = base + LA + LB * t
            for r in range(3):
                for j in range(4):
                    place = 64 * r + 16 * j
                    src, tile = start + ROWS + place % 48, place // 48
                    dst, col = 64 * (r // 2) + 16 * j, low + 128 * (r % 2)
                    left_ref[dst : dst + 16, col : col + 128] = b_ref[
                        src : src + 16, 128 * tile : 128 * (tile + 1)
                    ]
        if FA + FB * (t + 1) <= LA:
            left_sums = add_left(left_sums, FA + FB * t)
    arrive(g_copies)
    wg = wg_ref[...].reshape(HID2, D)
    wu = wu_ref[...].reshape(HID2, D)
    for low in range(LA, D, 512):
        left_sums = add_left(left_sums, low)
    gate_left, up_left = grads(
        *left_sums,
        (gates_ref[ROWS : ROWS + 128, 0:1], gates_ref[ROWS : ROWS + 128, 1:2]),
    )
    gate_grad, up_grad = grads(
        gate_pre, up_pre, back_proj, (gates_ref[0:ROWS, 0:1], gates_ref[0:ROWS, 1:2])
    )

    def part(low, width):
        cols = slice(low, low + width)
        return (
            dot(gate_grad, wg[:, cols]) + dot(up_grad, wu[:, cols]),
            dot(gate_left, wg[:, cols]) + dot(up_left, wu[:, cols]),
        )

    outs = []
    rests = []
    for q in range(RA // 512):
        sums, rest = part(512 * q, 512)
        send_ref[:, 512 * q : 512 * (q + 1)] = sums.astype(BF)
        rests.append(rest.astype(BF))
    for h in range(2):
        for s in range(2):
            for k in range(4):
                low = 256 * h + 32 * (4 * s + k)
                z_ref[low : low + 32, :] = rests[1][64 * s + 32 * h : 64 * s + 32 * h + 32, 128 * k : 128 * (k + 1)]
        rows = slice(256 * h, 256 * (h + 1))
        send_ref[rows, RA:BACK_A] = dot(turn_back, z_ref[rows, :]).astype(BF)
        for i in range(2 * h, 2 * h + 2):
            rows = pl.ds(128 * i, 128)
            outs.append(pltpu.make_async_copy(send_ref.at[rows], send_out.at[rows], out_sems.at[NT + i]))
            outs[-1].start()
    row = iota((256, 256), 0)
    col = iota((256, 256), 1)
    place_main = mask(((col >> 3) == (row >> 3)) & (((col & 7) >> 1) == (row & 7)))
    row = iota((ROWS, 256), 0)
    col = iota((ROWS, 256), 1)
    place_left = mask(((col & 63) == (row >> 3)) & ((row & 7) == 4 + (col >> 6)))

    def halves(tile, odd_rows, odd_slice):
        low_half = iota(tile.shape, 1) < 64
        moved = pltpu.roll(tile, 64, 1)
        both = jnp.where(low_half, moved, tile) if odd_slice else jnp.where(low_half, tile, moved)
        return jnp.where(low_half == odd_rows, 0.0, both).astype(BF)

    odd_main = (iota((ROWS, 128), 0) & 1) == 1
    odd_left = iota((128, 128), 0) >= 64
    for c in range(2):
        half_main, half_left = part(2048 + 256 * c, 256)
        for pair in range(2):
            t0 = 4 * c + 2 * pair
            full_main, full_left = part(RA + 128 * t0, 256)
            tile_main = half_main[:, 128 * pair : 128 * (pair + 1)]
            tile_left = half_left[:, 128 * pair : 128 * (pair + 1)]
            mains = jnp.concatenate([halves(tile_main, odd_main, i == 1) for i in range(2)], axis=1)
            halves_left = [halves(tile_left, odd_left, i == 1) for i in range(2)]
            extra = [
                rests[0][64 * (t // 4) : 64 * (t // 4) + 64, 128 * (t % 4) : 128 * (t % 4 + 1)]
                for t in (t0, t0 + 1)
            ]
            lefts = jnp.concatenate(
                [
                    full_left.astype(BF),
                    jnp.concatenate([half[0:64] + half[64:128] for half in halves_left], axis=1),
                    jnp.concatenate(extra, axis=1),
                ],
                axis=0,
            )
            placed = dot(place_left, lefts)
            for h in range(2):
                rows = slice(256 * h, 256 * (h + 1))
                both = (placed[rows] + dot(place_main, mains[rows])).astype(BF)
                for i in range(2):
                    rs_ref[t0 + i, rows, 128:256] = both[:, 128 * i : 128 * (i + 1)]
            for i in range(2):
                rs_ref[t0 + i, :, 0:128] = full_main[:, 128 * i : 128 * (i + 1)].astype(BF)
                outs.append(pltpu.make_async_copy(rs_ref.at[t0 + i], rs_out.at[t0 + i], out_sems.at[t0 + i]))
                outs[-1].start()
    for copy in outs:
        copy.wait()


def spread_positions(msg_ref):
    pos, _ = positions(msg_ref[:, FB + LB : FB + LB + META])
    row = iota((128, ROWS), 0)
    col = iota((128, ROWS), 1)
    pick = jnp.where(row == 2 * (col >> 3), 1.0, 0.0).astype(BF)
    return dot(pos.astype(BF), pick).astype(I32), col & 7


def combine_a_kernel(msg_ref, a_ref, out_ref):
    spread, sub = spread_positions(msg_ref)
    main = mask(spread == sub)
    total = dot(main, a_ref[:, 0:RA])
    out_ref[:, 0:512] = total[:, 0:512].astype(BF)
    for k in range(4):
        left = mask((spread == 8 + (sub >> 2)) & ((sub & 3) == k))
        low = 512 + 128 * k
        rest = dot(left, a_ref[:, RA:BACK_A])
        out_ref[:, low : low + 128] = (total[:, low : low + 128] + rest).astype(BF)


def combine_b_kernel(msg_ref, b_ref, a_ref, slice_ref, out_ref):
    spread, sub = spread_positions(msg_ref)
    main = mask(spread == sub)
    tile = b_ref[:, 128:256]
    rest = mask(((sub == 4) & (spread == 8)) | ((sub == 5) & (spread == 9)))
    full = dot(main, b_ref[:, 0:128]) + dot(rest, tile)
    low = dot(mask(((sub < 4) & (spread == 2 * sub)) | ((sub == 6) & (spread == 8))), tile)
    high = dot(mask(((sub < 4) & (spread == 2 * sub + 1)) | ((sub == 6) & (spread == 9))), tile)
    both = jnp.where(iota((NTOK, 128), 1) < 64, low, high)
    both = both + pltpu.roll(both, 64, 1)
    me = slice_ref[0, 0]
    extra = dot(mask((sub == 7) & (spread == 8 + (me >> 2))), tile)
    tiles = [
        a_ref[:, 128 * j : 128 * (j + 1)].astype(F32) + jnp.where((me & 3) == j, extra, 0.0)
        for j in range(4)
    ]
    tiles += [a_ref[:, 512:RA].astype(F32), full, both]
    values = jnp.concatenate([tile.astype(BF) for tile in tiles], axis=1)
    row = iota((64, NTOK), 0)
    col = iota((64, NTOK), 1)
    out_ref[:, 0:LAST] = dot(mask(col == 16 * (row >> 3) + (row & 7)), values).astype(BF)
    spread = [
        dot(mask((col == 16 * (row >> 3) + 8 + (row & 3)) & (((row >> 2) & 1) == i)), values)
        for i in range(2)
    ]
    for j in range(LAST // 256):
        packed = spread[0][:, 256 * j : 256 * j + 128] + spread[1][:, 256 * j + 128 : 256 * (j + 1)]
        out_ref[:, LAST + 128 * j : LAST + 128 * (j + 1)] = packed.astype(BF)


def finish_kernel(in_ref, out_ref):
    def tile(t, j):
        first = in_ref[t, :, 128 * j : 128 * (j + 1)].astype(F32)
        low = LAST + 128 * (j // 2)
        rest = in_ref[t, :, low : low + 128].astype(F32)
        return first, rest

    def store(low, first, rest, odd):
        rest = pltpu.roll(rest, 4, 0) if odd else rest
        out_ref[:, low : low + 128] = jnp.concatenate([first, rest], axis=0).astype(BF)[0:OWN]

    for j in range(RA // 128):
        first, rest = tile(0, j)
        for t in range(1, NT):
            more = tile(t, j)
            first, rest = first + more[0], rest + more[1]
        store(128 * j, first, rest, j % 2 == 1)
    for t in range(NT):
        store(RA + 128 * t, *tile(t, RA // 128), False)
    low_half = iota((8, 128), 1) < 64
    for t in range(0, NT, 2):
        pair = zip(tile(t, RA // 128 + 1), tile(t + 1, RA // 128 + 1))
        store(2048 + 64 * t, *[jnp.where(low_half, one, two) for one, two in pair], True)


def shape(*dims, dtype=BF):
    return jax.ShapeDtypeStruct(dims, dtype)


def per_device(tokens, out_grad, expert_ids, gate_values, gate_weight, up_weight, down_weight):
    weights = (gate_weight, up_weight, down_weight)
    lanes = FB + LB + META
    msg, both = call(start_kernel, (shape(NT, PADDED, lanes), shape(PADDED, 2 * D)), "start", limit=LARGE)(
        tokens, out_grad, expert_ids.T, gate_values.T
    )
    both_all = lax.all_gather(both, "tensor", axis=0, tiled=True)
    msg = lax.all_to_all(msg, "tensor", 0, 0, tiled=True).reshape(NTOK, lanes)
    send_b = call(pack_b_kernel, shape(ROWS, SENT_B), "pack_b", flops=2 * ROWS * 128 * 1280)(msg)
    recv_b = lax.all_to_all(send_b.reshape(NE, 8, SENT_B), "expert", 0, 0, tiled=True)
    recv_b = recv_b.reshape(ROWS, SENT_B)
    own_b = call(unpack_b_kernel, shape(GATHERED, FB), "unpack_b", flops=2 * ROWS * 256 * 128)(recv_b)
    all_b = lax.all_gather(own_b, "tensor", axis=0, tiled=True)
    send_a, gates = call(
        pack_a_kernel,
        (shape(ROWS, SENT_A), shape(ROWS + 128, 128, dtype=F32)),
        "pack_a",
        flops=2 * ROWS * 128 * 4096,
        scratch=[pltpu.VMEM((NTOK, 2 * D), BF), pltpu.SemaphoreType.DMA],
        ins=[VMEM, VMEM, HBM],
    )(msg, recv_b[:, FB:SENT_B], both_all)
    recv_a = lax.all_to_all(send_a.reshape(NE, 8, SENT_A), "expert", 0, 0, tiled=True)
    to_sum, to_send = call(
        experts_kernel,
        (shape(NT, ROWS, RB), shape(ROWS, BACK_A)),
        "experts",
        flops=10 * 640 * D * HID2,
        moved=13_000_000,
        scratch=[
            pltpu.VMEM((ROWS, SENT_A), BF),
            pltpu.VMEM((NT * GATHERED, FB), BF),
            pltpu.VMEM((ROWS + 128, 128), F32),
            pltpu.VMEM((2, HID2 // 2, D), BF),
            pltpu.VMEM((2, HID2 // 2, D), BF),
            pltpu.VMEM((2, HID2 // 2, D), BF),
            pltpu.VMEM((128, 2 * D), BF),
            pltpu.VMEM((ROWS, 128), BF),
            pltpu.VMEM((NT, ROWS, RB), BF),
            pltpu.VMEM((ROWS, BACK_A), BF),
            pltpu.SemaphoreType.DMA((36,)),
            pltpu.SemaphoreType.DMA((NT + 4,)),
        ],
        limit=LARGE,
        ins=[HBM] * 6,
        outs=(HBM, HBM),
    )(recv_a.reshape(ROWS, SENT_A), all_b, gates, *weights)
    summed = lax.psum_scatter(to_sum, "tensor", scatter_dimension=0, tiled=False)
    back_a = lax.all_to_all(to_send.reshape(NE, 8, BACK_A), "expert", 0, 0, tiled=True)
    back_b = lax.all_to_all(summed.reshape(NE, 8, RB), "expert", 0, 0, tiled=True)
    part_a = call(combine_a_kernel, shape(NTOK, RA), "combine_a", flops=2 * ROWS * 128 * 2048)(
        msg, back_a.reshape(ROWS, BACK_A)
    )
    me = lax.axis_index("tensor").astype(I32).reshape(1, 1)
    last = call(
        combine_b_kernel,
        shape(64, LAST_PACKED),
        "combine_b",
        flops=2 * ROWS * 128 * 1024,
        ins=[VMEM, VMEM, VMEM, pl.BlockSpec(memory_space=pltpu.SMEM)],
    )(msg, back_b.reshape(ROWS, RB), part_a, me)
    last = lax.all_to_all(last.reshape(NT, 8, LAST_PACKED), "tensor", 0, 0, tiled=True)
    return call(finish_kernel, shape(OWN, D), "finish")(last)


def solution(mesh):
    return jax.shard_map(
        per_device,
        mesh=mesh,
        in_specs=(
            P(("expert", "tensor"), None),
            P(("expert", "tensor"), None),
            P(("expert", "tensor"), None),
            P(("expert", "tensor"), None),
            P("expert", "tensor", None),
            P("expert", "tensor", None),
            P("expert", "tensor", None),
        ),
        out_specs=P(("expert", "tensor"), None),
        check_vma=False,
    )
```

```python
import jax
import jax.numpy as jnp
from jax import lax
from jax.experimental import pallas as pl
from jax.experimental.pallas import tpu as pltpu
from jax.sharding import PartitionSpec as P

BF = jnp.bfloat16
F32 = jnp.float32
I32 = jnp.int32
D = 2560
OWN = 12
PADDED = 16
NT = 8
NE = 64
NTOK = NT * PADDED
ROWS = NE * 8
HID2 = 192
FA = 512
FB = (D - FA) // 4
LA = 1536
LB = (D - LA) // 4
FOURTH = [D * (t // 4) + LA + LB * (t % 4) + 128 for t in range(8)]
META = 128
SENT_A = 2 * FA + 2 * 2 * LA // 8 + 128
SENT_B = FB + 128
GATHERED = ROWS + 48
RA = 1024
RB = 256
BACK_A = RA + 128
LAST = RA + RB
LAST_PACKED = LAST * 3 // 2
SMALL = 24 * 1024 * 1024
LARGE = 60 * 1024 * 1024


HBM = pl.BlockSpec(memory_space=pltpu.HBM)
VMEM = pl.BlockSpec(memory_space=pltpu.VMEM)


def call(kernel, out_shapes, name, flops=0, moved=0, scratch=(), limit=SMALL, ins=None, outs=None):
    specs = {}
    if ins is not None:
        specs["in_specs"] = ins
    if outs is not None:
        specs["out_specs"] = outs
    return pl.pallas_call(
        kernel,
        out_shape=out_shapes,
        **specs,
        scratch_shapes=scratch,
        name=name,
        cost_estimate=pl.CostEstimate(flops=flops, bytes_accessed=moved, transcendentals=0),
        compiler_params=pltpu.CompilerParams(vmem_limit_bytes=limit),
    )


def dot(a, b):
    return jnp.dot(a, b, preferred_element_type=F32)


def dot_t(a, b):
    return lax.dot_general(a, b, (((1,), (1,)), ((), ())), preferred_element_type=F32)


def iota(shape, dim):
    return lax.broadcasted_iota(I32, shape, dim)


def mask(cond):
    return jnp.where(cond, 1.0, 0.0).astype(BF)


def start_kernel(x_ref, dy_ref, ids_ref, gates_ref, msg_ref, all_ref):
    msg_ref[...] = jnp.zeros_like(msg_ref)
    all_ref[...] = jnp.zeros_like(all_ref)
    all_ref[0:OWN, 0:D] = x_ref[...]
    all_ref[0:OWN, D : 2 * D] = dy_ref[...]
    row = iota((6, META), 0)
    lane = iota((6, META), 1)
    place = [jnp.where(lane == row + 6 * i, 1.0, 0.0).astype(BF) for i in range(2)]
    cols = (((0,), (0,)), ((), ()))
    meta = lax.dot_general(
        ids_ref[...].astype(F32).astype(BF), place[0], cols, preferred_element_type=F32
    ) + lax.dot_general(gates_ref[...], place[1], cols, preferred_element_type=F32)
    meta = meta.astype(BF)
    for t in range(NT):
        src = x_ref if t < 4 else dy_ref
        low = FA + FB * (t % 4)
        msg_ref[t, 0:OWN, 0:FB] = src[:, low : low + FB]
        low = LA + LB * (t % 4)
        msg_ref[t, 0:OWN, FB : FB + LB] = src[:, low : low + LB]
        msg_ref[t, 0:OWN, FB + LB : FB + LB + META] = meta


def positions(meta):
    ids = meta.astype(F32).astype(I32)
    lane = iota((NTOK, 128), 1)
    row = iota((NTOK, 128), 0)
    hit = jnp.zeros((NTOK, 128), jnp.bool_)
    for k in range(6):
        hit = hit | ((ids[:, k : k + 1] >> 1) == (lane >> 1))
    member = jnp.where(hit & ((row & 15) < OWN), 1.0, 0.0)
    lower = jnp.where(lane < row, 1.0, 0.0).astype(BF)
    earlier = dot(lower, member.astype(BF))
    return jnp.where(member > 0.5, earlier, -1.0), ids


def one_hots(pos):
    row = iota((ROWS, 128), 0)
    lane = iota((ROWS, 128), 1)
    pick = jnp.where(lane == 2 * (row >> 3), 1.0, 0.0).astype(BF)
    spread = dot_t(pick, pos.astype(BF)).astype(I32)
    sub = row & 7
    main = jnp.where(spread == sub, 1.0, 0.0).astype(BF)
    left = jnp.where(spread == 8 + (sub >> 2), 1.0, 0.0).astype(BF)
    return main, left, mask(spread == 9)


def pack_b_kernel(msg_ref, out_ref):
    meta = msg_ref[:, FB + LB : FB + LB + META]
    pos, ids = positions(meta)
    main, left, _ = one_hots(pos)
    out_ref[:, 0:FB] = dot(main, msg_ref[:, 0:FB]).astype(BF)
    row = iota((ROWS, 128), 0)
    sub = row & 7
    pick = mask(iota((ROWS, 128), 1) == 2 * (row >> 3))
    spread = dot_t(pick, pos.astype(BF)).astype(I32)
    tiles = dot(mask(spread == 8 + (sub >> 1)), msg_ref[:, FB : FB + LB])
    tile = jnp.where((sub & 1) == 0, tiles[:, 0:128], tiles[:, 128:256])
    gates = meta.astype(F32)
    lane = iota((NTOK, 128), 1)
    weight = jnp.zeros((NTOK, 128), F32)
    for k in range(6):
        weight = weight + jnp.where(ids[:, k : k + 1] == lane, gates[:, 6 + k : 7 + k], 0.0)
    row16 = iota((16, 128), 0)
    gate_of = jnp.zeros((16, 128), F32)
    for s in range(10):
        col = jnp.sum(jnp.where(pos == float(s), weight, 0.0), axis=0, keepdims=True)
        gate_of = jnp.where(row16 == s, col, gate_of)
    gate_of = jnp.concatenate([gate_of, jnp.zeros((112, 128), F32)], axis=0).astype(BF)
    pick = mask((iota((ROWS, 128), 1) == 2 * (row >> 3) + (sub & 1)) & ((sub >> 1) == 2))
    out_ref[:, FB : FB + 128] = jnp.where(sub < 4, tile, dot_t(pick, gate_of)).astype(BF)


def unpack_b_kernel(in_ref, out_ref):
    out_ref[0:ROWS, :] = in_ref[:, 0:FB]
    turn = perm(False)[0:96]
    for h in range(2):
        turned = dot(turn, in_ref[256 * h : 256 * (h + 1), FB : FB + 128]).astype(BF)
        for r in range(3):
            for j in range(2):
                place = 64 * r + 32 * h + 16 * j
                low, tile = ROWS + place % 48, place // 48
                out_ref[low : low + 16, 128 * tile : 128 * (tile + 1)] = turned[
                    32 * r + 16 * j : 32 * r + 16 * (j + 1)
                ]


def gates_as_columns(tile_ref, gate_ref):
    turn = perm(False)[128:192]
    turned = [dot(turn, tile_ref[256 * h : 256 * (h + 1), :]) for h in range(2)]
    spread = mask((iota((ROWS, 64), 0) >> 3) == iota((ROWS, 64), 1))
    wide = iota((ROWS, 128), 1)
    sub = iota((ROWS, 128), 0) & 7
    main = jnp.zeros((ROWS, 128), F32)
    rest = jnp.zeros((128, 128), F32)
    lane = iota((128, 128), 1)
    for e in range(2):
        own = jnp.concatenate([part[32 * e : 32 * (e + 1)] for part in turned], axis=0)
        both = jnp.where(wide == sub, dot(spread, own.astype(BF)), 0.0)
        main = jnp.where(wide == e, jnp.sum(both, axis=1, keepdims=True), main)
        column = jnp.concatenate([own[:, 8:9], own[:, 9:10]], axis=0)
        rest = jnp.where(lane == e, column, rest)
    gate_ref[0:ROWS, :] = main
    gate_ref[ROWS : ROWS + 128, :] = rest


def pack_a_kernel(msg_ref, tile_ref, x_in, send_out, gate_out, x_ref, out_ref, gate_ref, sems, out_sems):
    copies = []
    for i in range(2 * D // 512):
        part = (slice(None), pl.ds(512 * i, 512))
        copies.append(pltpu.make_async_copy(x_in.at[part], x_ref.at[part], sems.at[i]))
        copies[-1].start()
    outs = []

    def send(src, dst):
        outs.append(pltpu.make_async_copy(src, dst, out_sems.at[len(outs)]))
        outs[-1].start()

    def send_lanes(low, width):
        part = (slice(None), pl.ds(low, width))
        send(out_ref.at[part], send_out.at[part])

    gates_as_columns(tile_ref, gate_ref)
    send(gate_ref, gate_out)
    pos, _ = positions(msg_ref[:, FB + LB : FB + LB + META])
    main, left, last = one_hots(pos)
    sub4 = iota((ROWS, 128), 0) & 3
    for copy in copies:
        copy.wait()
    for part in range(2):
        out_ref[:, part * FA : (part + 1) * FA] = dot(main, x_ref[:, part * D : part * D + FA]).astype(BF)
        send_lanes(part * FA, FA)
        for q in range(LA // 512):
            low = part * D + 512 * q
            spread = dot(left, x_ref[:, low : low + 512])
            out = spread[:, 0:128]
            for k in range(1, 4):
                out = jnp.where(sub4 == k, spread[:, 128 * k : 128 * (k + 1)], out)
            low = 2 * FA + 128 * (part * (LA // 512) + q)
            out_ref[:, low : low + 128] = out.astype(BF)
    sub = iota((ROWS, 128), 0) & 7
    out = jnp.zeros((ROWS, 128), F32)
    for r in range(8):
        low = FOURTH[r]
        out = jnp.where(sub == r, dot(last, x_ref[:, low : low + 128]), out)
    out_ref[:, SENT_A - 128 : SENT_A] = out.astype(BF)
    send_lanes(2 * FA, SENT_A - 2 * FA)
    for copy in outs:
        copy.wait()


def perm(inverse):
    row = iota((256, 256), 0)
    col = iota((256, 256), 1)
    if inverse:
        row, col = col, row
    return mask(((col & 7) == (row >> 5)) & ((col >> 3) == (row & 31)))


def grads(gate_pre, up_pre, back_proj, gates):
    lane = iota(gate_pre.shape, 1)
    scaled = back_proj * jnp.where(lane < HID2 // 2, gates[0], gates[1])
    sig = 1.0 / (1.0 + jnp.exp(-gate_pre))
    up_grad = (scaled * gate_pre * sig).astype(BF)
    gate_grad = (scaled * up_pre * sig * (1.0 + gate_pre * (1.0 - sig))).astype(BF)
    return gate_grad, up_grad


def experts_kernel(
    a_in,
    b_in,
    gates_in,
    wg_in,
    wu_in,
    wd_in,
    rs_out,
    send_out,
    a_ref,
    b_ref,
    gates_ref,
    wg_ref,
    wu_ref,
    wd_ref,
    left_ref,
    z_ref,
    rs_ref,
    send_ref,
    sems,
    out_sems,
):
    started = []

    def fetch(src, dst, parts):
        copies = []
        for part in parts:
            copies.append(pltpu.make_async_copy(src.at[part], dst.at[part], sems.at[len(started)]))
            copies[-1].start()
            started.append(copies[-1])
        return copies

    def fetch_weights(low):
        part = (slice(None), slice(None), pl.ds(low, 512))
        return [
            copy
            for src, dst in ((wg_in, wg_ref), (wu_in, wu_ref), (wd_in, wd_ref))
            for copy in fetch(src, dst, [part])
        ]

    def arrive(copies):
        for copy in copies:
            copy.wait()

    every = slice(None)
    left_copies = fetch(
        a_in, a_ref, [(pl.ds(256 * h, 256), pl.ds(2 * FA, SENT_A - 2 * FA)) for h in range(2)]
    )
    main_copies = fetch(a_in, a_ref, [(every, pl.ds(FA * i, FA)) for i in range(2)]) + fetch_weights(0)
    b_copies = [
        fetch(b_in, b_ref, [pl.ds(GATHERED * u + 272 * i, 272 + 16 * i) for u in (t, t + 4) for i in range(2)])
        + fetch_weights(FA + FB * t)
        for t in range(4)
    ]
    g_copies = fetch(gates_in, gates_ref, [pl.ds(0, ROWS + 128)])
    turn = perm(False)
    turn_back = perm(True)
    arrive(left_copies)
    for h in range(2):
        turned = dot(turn, a_ref[256 * h : 256 * (h + 1), 2 * FA : SENT_A]).astype(BF)
        for q in range(2 * LA // 512):
            base = (q // (LA // 512)) * D + 512 * (q % (LA // 512))
            for s in range(2):
                for k in range(4):
                    low = 64 * s + 32 * h
                    left_ref[low : low + 32, base + 128 * k : base + 128 * (k + 1)] = turned[
                        32 * (4 * s + k) : 32 * (4 * s + k + 1), 128 * q : 128 * (q + 1)
                    ]
        for r in range(8):
            low = 64 + 32 * h
            left_ref[low : low + 32, FOURTH[r] : FOURTH[r] + 128] = turned[
                32 * r : 32 * (r + 1), 4 * LA // 8 : 4 * LA // 8 + 128
            ]
    arrive(main_copies)

    def block(ref, low):
        return ref[:, :, low : low + 512].reshape(HID2, 512)

    def add_left(sums, low):
        rows = left_ref[:, low : low + 512]
        products = (
            dot_t(rows, block(wg_ref, low)),
            dot_t(rows, block(wu_ref, low)),
            dot_t(left_ref[:, D + low : D + low + 512], block(wd_ref, low)),
        )
        return [a + b for a, b in zip(sums, products)]

    left_sums = add_left([0.0] * 3, 0)
    gate_pre = dot_t(a_ref[:, 0:FA], block(wg_ref, 0))
    up_pre = dot_t(a_ref[:, 0:FA], block(wu_ref, 0))
    back_proj = dot_t(a_ref[:, FA : 2 * FA], block(wd_ref, 0))
    for t in range(4):
        arrive(b_copies[t])
        low = FA + FB * t
        x0, y0 = GATHERED * t, GATHERED * (t + 4)
        rows = b_ref[x0 : x0 + ROWS, :]
        gate_pre = gate_pre + dot_t(rows, block(wg_ref, low))
        up_pre = up_pre + dot_t(rows, block(wu_ref, low))
        back_proj = back_proj + dot_t(b_ref[y0 : y0 + ROWS, :], block(wd_ref, low))
        for base, start in ((0, x0), (D, y0)):
            low = base + LA + LB * t
            for r in range(3):
                for j in range(4):
                    place = 64 * r + 16 * j
                    src, tile = start + ROWS + place % 48, place // 48
                    dst, col = 64 * (r // 2) + 16 * j, low + 128 * (r % 2)
                    left_ref[dst : dst + 16, col : col + 128] = b_ref[
                        src : src + 16, 128 * tile : 128 * (tile + 1)
                    ]
        if FA + FB * (t + 1) <= LA:
            left_sums = add_left(left_sums, FA + FB * t)
    arrive(g_copies)
    wg = wg_ref[...].reshape(HID2, D)
    wu = wu_ref[...].reshape(HID2, D)
    for low in range(LA, D, 512):
        left_sums = add_left(left_sums, low)
    gate_left, up_left = grads(
        *left_sums,
        (gates_ref[ROWS : ROWS + 128, 0:1], gates_ref[ROWS : ROWS + 128, 1:2]),
    )
    gate_grad, up_grad = grads(
        gate_pre, up_pre, back_proj, (gates_ref[0:ROWS, 0:1], gates_ref[0:ROWS, 1:2])
    )

    def part(low, width):
        cols = slice(low, low + width)
        return (
            dot(gate_grad, wg[:, cols]) + dot(up_grad, wu[:, cols]),
            dot(gate_left, wg[:, cols]) + dot(up_left, wu[:, cols]),
        )

    outs = []
    rests = []
    for q in range(RA // 512):
        sums, rest = part(512 * q, 512)
        send_ref[:, 512 * q : 512 * (q + 1)] = sums.astype(BF)
        rests.append(rest.astype(BF))
    for h in range(2):
        for s in range(2):
            for k in range(4):
                low = 256 * h + 32 * (4 * s + k)
                z_ref[low : low + 32, :] = rests[1][64 * s + 32 * h : 64 * s + 32 * h + 32, 128 * k : 128 * (k + 1)]
        rows = slice(256 * h, 256 * (h + 1))
        send_ref[rows, RA:BACK_A] = dot(turn_back, z_ref[rows, :]).astype(BF)
        for i in range(2 * h, 2 * h + 2):
            rows = pl.ds(128 * i, 128)
            outs.append(pltpu.make_async_copy(send_ref.at[rows], send_out.at[rows], out_sems.at[NT + i]))
            outs[-1].start()
    row = iota((256, 256), 0)
    col = iota((256, 256), 1)
    place_main = mask(((col >> 3) == (row >> 3)) & (((col & 7) >> 1) == (row & 7)))
    row = iota((ROWS, 256), 0)
    col = iota((ROWS, 256), 1)
    place_left = mask(((col & 63) == (row >> 3)) & ((row & 7) == 4 + (col >> 6)))

    def halves(tile, odd_rows, odd_slice):
        low_half = iota(tile.shape, 1) < 64
        moved = pltpu.roll(tile, 64, 1)
        both = jnp.where(low_half, moved, tile) if odd_slice else jnp.where(low_half, tile, moved)
        return jnp.where(low_half == odd_rows, 0.0, both).astype(BF)

    odd_main = (iota((ROWS, 128), 0) & 1) == 1
    odd_left = iota((128, 128), 0) >= 64
    for c in range(2):
        half_main, half_left = part(2048 + 256 * c, 256)
        for pair in range(2):
            t0 = 4 * c + 2 * pair
            full_main, full_left = part(RA + 128 * t0, 256)
            tile_main = half_main[:, 128 * pair : 128 * (pair + 1)]
            tile_left = half_left[:, 128 * pair : 128 * (pair + 1)]
            mains = jnp.concatenate([halves(tile_main, odd_main, i == 1) for i in range(2)], axis=1)
            halves_left = [halves(tile_left, odd_left, i == 1) for i in range(2)]
            extra = [
                rests[0][64 * (t // 4) : 64 * (t // 4) + 64, 128 * (t % 4) : 128 * (t % 4 + 1)]
                for t in (t0, t0 + 1)
            ]
            lefts = jnp.concatenate(
                [
                    full_left.astype(BF),
                    jnp.concatenate([half[0:64] + half[64:128] for half in halves_left], axis=1),
                    jnp.concatenate(extra, axis=1),
                ],
                axis=0,
            )
            placed = dot(place_left, lefts)
            for h in range(2):
                rows = slice(256 * h, 256 * (h + 1))
                both = (placed[rows] + dot(place_main, mains[rows])).astype(BF)
                for i in range(2):
                    rs_ref[t0 + i, rows, 128:256] = both[:, 128 * i : 128 * (i + 1)]
            for i in range(2):
                rs_ref[t0 + i, :, 0:128] = full_main[:, 128 * i : 128 * (i + 1)].astype(BF)
                outs.append(pltpu.make_async_copy(rs_ref.at[t0 + i], rs_out.at[t0 + i], out_sems.at[t0 + i]))
                outs[-1].start()
    for copy in outs:
        copy.wait()


def spread_positions(msg_ref):
    pos, _ = positions(msg_ref[:, FB + LB : FB + LB + META])
    row = iota((128, ROWS), 0)
    col = iota((128, ROWS), 1)
    pick = jnp.where(row == 2 * (col >> 3), 1.0, 0.0).astype(BF)
    return dot(pos.astype(BF), pick).astype(I32), col & 7


def combine_a_kernel(msg_ref, a_ref, out_ref):
    spread, sub = spread_positions(msg_ref)
    main = mask(spread == sub)
    total = dot(main, a_ref[:, 0:RA])
    out_ref[:, 0:512] = total[:, 0:512].astype(BF)
    for k in range(4):
        left = mask((spread == 8 + (sub >> 2)) & ((sub & 3) == k))
        low = 512 + 128 * k
        rest = dot(left, a_ref[:, RA:BACK_A])
        out_ref[:, low : low + 128] = (total[:, low : low + 128] + rest).astype(BF)


def combine_b_kernel(msg_ref, b_ref, a_ref, slice_ref, out_ref):
    spread, sub = spread_positions(msg_ref)
    main = mask(spread == sub)
    tile = b_ref[:, 128:256]
    rest = mask(((sub == 4) & (spread == 8)) | ((sub == 5) & (spread == 9)))
    full = dot(main, b_ref[:, 0:128]) + dot(rest, tile)
    low = dot(mask(((sub < 4) & (spread == 2 * sub)) | ((sub == 6) & (spread == 8))), tile)
    high = dot(mask(((sub < 4) & (spread == 2 * sub + 1)) | ((sub == 6) & (spread == 9))), tile)
    both = jnp.where(iota((NTOK, 128), 1) < 64, low, high)
    both = both + pltpu.roll(both, 64, 1)
    me = slice_ref[0, 0]
    extra = dot(mask((sub == 7) & (spread == 8 + (me >> 2))), tile)
    tiles = [
        a_ref[:, 128 * j : 128 * (j + 1)].astype(F32) + jnp.where((me & 3) == j, extra, 0.0)
        for j in range(4)
    ]
    tiles += [a_ref[:, 512:RA].astype(F32), full, both]
    values = jnp.concatenate([tile.astype(BF) for tile in tiles], axis=1)
    row = iota((64, NTOK), 0)
    col = iota((64, NTOK), 1)
    out_ref[:, 0:LAST] = dot(mask(col == 16 * (row >> 3) + (row & 7)), values).astype(BF)
    spread = [
        dot(mask((col == 16 * (row >> 3) + 8 + (row & 3)) & (((row >> 2) & 1) == i)), values)
        for i in range(2)
    ]
    for j in range(LAST // 256):
        packed = spread[0][:, 256 * j : 256 * j + 128] + spread[1][:, 256 * j + 128 : 256 * (j + 1)]
        out_ref[:, LAST + 128 * j : LAST + 128 * (j + 1)] = packed.astype(BF)


def finish_kernel(in_ref, out_ref):
    def tile(t, j):
        first = in_ref[t, :, 128 * j : 128 * (j + 1)].astype(F32)
        low = LAST + 128 * (j // 2)
        rest = in_ref[t, :, low : low + 128].astype(F32)
        return first, rest

    def store(low, first, rest, odd):
        rest = pltpu.roll(rest, 4, 0) if odd else rest
        out_ref[:, low : low + 128] = jnp.concatenate([first, rest], axis=0).astype(BF)[0:OWN]

    for j in range(RA // 128):
        first, rest = tile(0, j)
        for t in range(1, NT):
            more = tile(t, j)
            first, rest = first + more[0], rest + more[1]
        store(128 * j, first, rest, j % 2 == 1)
    for t in range(NT):
        store(RA + 128 * t, *tile(t, RA // 128), False)
    low_half = iota((8, 128), 1) < 64
    for t in range(0, NT, 2):
        pair = zip(tile(t, RA // 128 + 1), tile(t + 1, RA // 128 + 1))
        store(2048 + 64 * t, *[jnp.where(low_half, one, two) for one, two in pair], True)


def shape(*dims, dtype=BF):
    return jax.ShapeDtypeStruct(dims, dtype)


def per_device(tokens, out_grad, expert_ids, gate_values, gate_weight, up_weight, down_weight):
    weights = (gate_weight, up_weight, down_weight)
    lanes = FB + LB + META
    msg, both = call(start_kernel, (shape(NT, PADDED, lanes), shape(PADDED, 2 * D)), "start", limit=LARGE)(
        tokens, out_grad, expert_ids.T, gate_values.T
    )
    both_all = lax.all_gather(both, "tensor", axis=0, tiled=True)
    msg = lax.all_to_all(msg, "tensor", 0, 0, tiled=True).reshape(NTOK, lanes)
    send_b = call(pack_b_kernel, shape(ROWS, SENT_B), "pack_b", flops=2 * ROWS * 128 * 1280)(msg)
    recv_b = lax.all_to_all(send_b.reshape(NE, 8, SENT_B), "expert", 0, 0, tiled=True)
    recv_b = recv_b.reshape(ROWS, SENT_B)
    own_b = call(unpack_b_kernel, shape(GATHERED, FB), "unpack_b", flops=2 * ROWS * 256 * 128)(recv_b)
    all_b = lax.all_gather(own_b, "tensor", axis=0, tiled=True)
    send_a, gates = call(
        pack_a_kernel,
        (shape(ROWS, SENT_A), shape(ROWS + 128, 128, dtype=F32)),
        "pack_a",
        flops=2 * ROWS * 128 * 4096,
        scratch=[
            pltpu.VMEM((NTOK, 2 * D), BF),
            pltpu.VMEM((ROWS, SENT_A), BF),
            pltpu.VMEM((ROWS + 128, 128), F32),
            pltpu.SemaphoreType.DMA((2 * D // 512,)),
            pltpu.SemaphoreType.DMA((4,)),
        ],
        limit=LARGE,
        ins=[VMEM, VMEM, HBM],
        outs=(HBM, HBM),
    )(msg, recv_b[:, FB:SENT_B], both_all)
    recv_a = lax.all_to_all(send_a.reshape(NE, 8, SENT_A), "expert", 0, 0, tiled=True)
    to_sum, to_send = call(
        experts_kernel,
        (shape(NT, ROWS, RB), shape(ROWS, BACK_A)),
        "experts",
        flops=10 * 640 * D * HID2,
        moved=13_000_000,
        scratch=[
            pltpu.VMEM((ROWS, SENT_A), BF),
            pltpu.VMEM((NT * GATHERED, FB), BF),
            pltpu.VMEM((ROWS + 128, 128), F32),
            pltpu.VMEM((2, HID2 // 2, D), BF),
            pltpu.VMEM((2, HID2 // 2, D), BF),
            pltpu.VMEM((2, HID2 // 2, D), BF),
            pltpu.VMEM((128, 2 * D), BF),
            pltpu.VMEM((ROWS, 128), BF),
            pltpu.VMEM((NT, ROWS, RB), BF),
            pltpu.VMEM((ROWS, BACK_A), BF),
            pltpu.SemaphoreType.DMA((36,)),
            pltpu.SemaphoreType.DMA((NT + 4,)),
        ],
        limit=LARGE,
        ins=[HBM] * 6,
        outs=(HBM, HBM),
    )(recv_a.reshape(ROWS, SENT_A), all_b, gates, *weights)
    summed = lax.psum_scatter(to_sum, "tensor", scatter_dimension=0, tiled=False)
    back_a = lax.all_to_all(to_send.reshape(NE, 8, BACK_A), "expert", 0, 0, tiled=True)
    back_b = lax.all_to_all(summed.reshape(NE, 8, RB), "expert", 0, 0, tiled=True)
    part_a = call(combine_a_kernel, shape(NTOK, RA), "combine_a", flops=2 * ROWS * 128 * 2048)(
        msg, back_a.reshape(ROWS, BACK_A)
    )
    me = lax.axis_index("tensor").astype(I32).reshape(1, 1)
    last = call(
        combine_b_kernel,
        shape(64, LAST_PACKED),
        "combine_b",
        flops=2 * ROWS * 128 * 1024,
        ins=[VMEM, VMEM, VMEM, pl.BlockSpec(memory_space=pltpu.SMEM)],
    )(msg, back_b.reshape(ROWS, RB), part_a, me)
    last = lax.all_to_all(last.reshape(NT, 8, LAST_PACKED), "tensor", 0, 0, tiled=True)
    return call(finish_kernel, shape(OWN, D), "finish")(last)


def solution(mesh):
    return jax.shard_map(
        per_device,
        mesh=mesh,
        in_specs=(
            P(("expert", "tensor"), None),
            P(("expert", "tensor"), None),
            P(("expert", "tensor"), None),
            P(("expert", "tensor"), None),
            P("expert", "tensor", None),
            P("expert", "tensor", None),
            P("expert", "tensor", None),
        ),
        out_specs=P(("expert", "tensor"), None),
        check_vma=False,
    )
```
